256 devices in a mesh: snap: 64 (over z, x, core), feat: 4 (over y).
Axes of the slice: x: 4, y: 4, z: 8, core: 2. Of those that a mesh axis runs over, the one named last changes fastest.
Arguments:
- node_features: bfloat16 [128, 4096, 256], P('snap', None, 'feat'), may hold values from -6 to 6
- tile_rows: int32 [128, 64], P('snap'), may hold values from 0 to 31
- tile_cols: int32 [128, 64], P('snap'), may hold values from 0 to 31, as said below
- tile_counts: int32 [128], P('snap'), may hold values from 4 to 64, as said below
- tile_values: bfloat16 [128, 64, 128, 128], P('snap'), may hold values from -0.5 to 0.5
- layer_one: bfloat16 [256, 256], replicated, may hold values from -0.375 to 0.375
- layer_two: bfloat16 [256, 256], replicated, may hold values from -0.375 to 0.375
- query_weight: bfloat16 [256, 256], replicated, may hold values from -1.25 to 1.25
- key_weight: bfloat16 [256, 256], replicated, may hold values from -1.25 to 1.25
- value_weight: bfloat16 [256, 256], replicated, may hold values from -0.375 to 0.375
- out_weight: bfloat16 [256, 256], replicated, may hold values from -0.375 to 0.375
Outputs:
- evolved: bfloat16 [128, 4096, 256], P('snap', None, 'feat')
The draws below stay inside these ranges and needn't reach their ends.
Inputs may be any that keep to these rules, and one draw needn't show every extreme that they name: `tile_cols`: block columns of the tile slots; a coordinate pair may be listed more than once, and such tiles add. `tile_counts`: some snapshot uses all 64 slots.
All inputs are finite; a program needn't handle non-finite values.
Results may differ from the reference program's by a relative error of at most 0.02.
The reference program's roundings to bfloat16 on the way count: a program that leaves them out, or rounds other values in their place, can miss the bound.
Values may be sent and summed in bfloat16 or wider, within the bound.
No kernel may reach another device: no remote copies, remote signals or barrier semaphores. Data moves between devices by JAX's collectives and lax.ppermute only.
A program may use at most 64 MiB of HBM per device.

```python
import jax
import jax.numpy as jnp
from jax import lax

D = 256
HEADS = 8
TILE = 128
HEAD_DIM = 32
SNAPS = 128
VERT = 4096
BLOCKS = 32
MAXT = 64
N_SNAP = 64


def tile_lists(key):
    row_ids = jax.random.randint(jax.random.fold_in(key, 101), (SNAPS, MAXT), 0, BLOCKS)
    col_ids = jax.random.randint(jax.random.fold_in(key, 102), (SNAPS, MAXT), 0, BLOCKS)
    levels = jax.random.randint(jax.random.fold_in(key, 103), (SNAPS,), 0, 11)
    counts = 4 + (MAXT - 4) * levels * levels * levels // 1000
    full_snapshot = jax.random.randint(jax.random.fold_in(key, 104), (), 0, SNAPS)
    counts = jnp.where(jnp.arange(SNAPS) == full_snapshot, MAXT, counts)
    return (row_ids.astype(jnp.int32), col_ids.astype(jnp.int32), counts.astype(jnp.int32))


def draw_tile_rows(key, part):
    return tile_lists(key)[0]


def draw_tile_cols(key, part):
    return tile_lists(key)[1]


def draw_tile_counts(key, part):
    return tile_lists(key)[2]


def attention_pair(key, which):
    separate = jnp.clip(jax.random.normal(jax.random.fold_in(key, 202 + which), (D, D), jnp.float32), -5.0, 5.0)
    combined = separate
    return (combined * D ** (-0.5)).astype(jnp.bfloat16)


def draw_query_weight(key, part):
    return attention_pair(key, 0)


def draw_key_weight(key, part):
    return attention_pair(key, 1)


def block_scale(rng, dims, split, smallest, largest):
    loudness = 1.0
    for axis_at, shards_of in split:
        draws = jax.random.uniform(jax.random.fold_in(jax.random.fold_in(rng, 6), axis_at), (shards_of,), jnp.float32, smallest / len(split), largest / len(split))
        loudness = loudness * jnp.repeat(jnp.exp(draws), dims[axis_at] // shards_of).reshape((-1,) + (1,) * (len(dims) - 1 - axis_at))
    return loudness


def normal_values(key, extent, spread, limit, split=(), kind=jnp.bfloat16):
    array = spread * jax.random.normal(key, extent, jnp.float32)
    if split:
        array = array * block_scale(key, extent, split, -0.22, 0.18)
    return jnp.clip(array, -limit, limit).astype(kind)


def setup_inputs(seed: int = 0) -> dict:
    splits = jax.random.split(jax.random.key(seed), 12)
    return {
        "node_features": normal_values(splits[0], (SNAPS, VERT, D), 1.0, 6.0, ((0, 64), (2, 4))),
        "tile_rows": draw_tile_rows(jax.random.fold_in(splits[11], 71), 0),
        "tile_cols": draw_tile_cols(jax.random.fold_in(splits[11], 71), 0),
        "tile_counts": draw_tile_counts(jax.random.fold_in(splits[11], 71), 0),
        "tile_values": normal_values(splits[4], (SNAPS, MAXT, TILE, TILE), TILE ** -0.5, 0.5, ((0, 64),)),
        "layer_one": normal_values(splits[5], (D, D), D ** -0.5, 0.375),
        "layer_two": normal_values(splits[6], (D, D), D ** -0.5, 0.375),
        "query_weight": draw_query_weight(jax.random.fold_in(splits[11], 71), 0),
        "key_weight": draw_key_weight(jax.random.fold_in(splits[11], 71), 0),
        "value_weight": normal_values(splits[9], (D, D), D ** -0.5, 0.375),
        "out_weight": normal_values(splits[10], (D, D), D ** -0.5, 0.375),
    }


masked_score = -1.0e30


def spread_snapshot(features, tile_block, block_rows, block_cols, slot_count):
    feat_width = features.shape[1]
    blocked = features.reshape(BLOCKS, TILE, feat_width)
    picked_blocks = blocked[block_cols]
    live_slots = (jnp.arange(MAXT, dtype=jnp.int32) < slot_count)
    products = jnp.einsum("irc,icf->irf", tile_block.astype(jnp.float32), picked_blocks.astype(jnp.float32), precision=lax.Precision.HIGHEST)
    products = products * live_slots.astype(jnp.float32)[:, None, None]
    membership = ((block_rows[None, :] == jnp.arange(BLOCKS, dtype=jnp.int32)[:, None]) & live_slots[None, :]).astype(jnp.float32)
    summed = jnp.dot(membership, products.reshape(MAXT, TILE * feat_width), precision=lax.Precision.HIGHEST)
    return summed.reshape(VERT, feat_width).astype(jnp.bfloat16)


def attend_block(hidden, query_weight, key_weight, value_weight, out_weight):
    snaps, verts, model_width = hidden.shape
    flat = hidden.reshape(snaps * verts, model_width)

    def project(weight):
        return jnp.dot(flat, weight, preferred_element_type=jnp.float32).astype(jnp.bfloat16).reshape(snaps, verts, HEADS, HEAD_DIM)

    query_heads = project(query_weight)
    key_heads = project(key_weight)
    value_heads = project(value_weight)
    scores = jnp.einsum("tvhd,uvhd->vhtu", query_heads.astype(jnp.float32), key_heads.astype(jnp.float32)) * (HEAD_DIM ** -0.5)
    causal = jnp.arange(snaps, dtype=jnp.int32)[:, None] >= jnp.arange(snaps, dtype=jnp.int32)[None, :]
    scores = jnp.where(causal, scores, masked_score)
    row_max = jnp.max(scores, axis=-1, keepdims=True)
    lifted = jnp.exp(scores - row_max)
    weights = (lifted / jnp.sum(lifted, axis=-1, keepdims=True)).astype(jnp.bfloat16)
    context = jnp.einsum("vhtu,uvhd->tvhd", weights.astype(jnp.float32), value_heads.astype(jnp.float32)).astype(jnp.bfloat16)
    context = context.reshape(snaps * verts, model_width)
    result = flat.astype(jnp.float32) + jnp.dot(context, out_weight, preferred_element_type=jnp.float32)
    return result.astype(jnp.bfloat16).reshape(snaps, verts, model_width)


def reference(node_features, tile_rows, tile_cols, tile_counts, tile_values, layer_one, layer_two, query_weight, key_weight, value_weight, out_weight):
    def evolve_snapshot(packed):
        features, tile_block, block_rows, block_cols, slot_count = packed
        spread_one = spread_snapshot(features, tile_block, block_rows, block_cols, slot_count)
        mixed_one = jnp.dot(spread_one, layer_one, preferred_element_type=jnp.float32)
        hidden_one = (features.astype(jnp.float32) + jnp.maximum(mixed_one, 0.0)).astype(jnp.bfloat16)
        spread_two = spread_snapshot(hidden_one, tile_block, block_rows, block_cols, slot_count)
        mixed_two = jnp.dot(spread_two, layer_two, preferred_element_type=jnp.float32)
        return (hidden_one.astype(jnp.float32) + jnp.maximum(mixed_two, 0.0)).astype(jnp.bfloat16)

    hidden_two = lax.map(evolve_snapshot, (node_features, tile_values, tile_rows, tile_cols, tile_counts))
    vert_block = VERT // N_SNAP
    grouped = hidden_two.reshape(SNAPS, N_SNAP, vert_block, D).transpose(1, 0, 2, 3)

    def attend_group(hidden):
        return attend_block(hidden, query_weight, key_weight, value_weight, out_weight)

    attended = lax.map(attend_group, grouped)
    return attended.transpose(1, 0, 2, 3).reshape(SNAPS, VERT, D)
```

```python
import functools

import jax
import jax.numpy as jnp
from jax import lax
from jax.experimental import pallas as pl
from jax.experimental.pallas import tpu as pltpu
from jax.sharding import PartitionSpec as P

HEADS = 8
HEAD_DIM = 32
TILE = 128
D = 256
SNAPS = 128
VERT = 4096
BLOCKS = 32
MAXT = 64
F_DEV = 4
S_DEV = 64
F_W = D // F_DEV
V_F = VERT // F_DEV
V_S = V_F // S_DEV
GROUP = 8

masked_score = -1e30
f32 = jnp.float32
bf16 = jnp.bfloat16
NT = (((1,), (1,)), ((), ()))
MIB = 2**20


def params(mib):
    return pltpu.CompilerParams(vmem_limit_bytes=mib * MIB)


def spread_kernel(chunked, counts, rows, cols, x_ref, tiles_ref, out_ref, acc):
    t = pl.program_id(0)
    acc[...] = jnp.zeros_like(acc)
    n = counts[t]

    def group(g, _):
        products = []
        for j in range(GROUP):
            i = g * GROUP + j
            col = cols[t, i]
            if chunked:
                x = x_ref[col // 8, 0, :, pl.ds(pl.multiple_of((col % 8) * TILE, TILE), TILE)]
            else:
                x = x_ref[0, :, pl.ds(pl.multiple_of(col * TILE, TILE), TILE)]
            products.append(
                lax.dot_general(x, tiles_ref[0, i], NT, preferred_element_type=f32)
            )
        for j in range(GROUP):
            i = g * GROUP + j
            row = jnp.where(i < n, rows[t, i], BLOCKS)
            acc[row] += products[j]
        return 0

    lax.fori_loop(0, (n + GROUP - 1) // GROUP, group, 0)
    for b in range(BLOCKS):
        out_ref[b // 8, 0, :, (b % 8) * TILE : (b % 8 + 1) * TILE] = acc[b].astype(bf16)


def spread(x, tiles, rows, cols, counts, chunked):
    if chunked:
        x_spec = pl.BlockSpec((F_DEV, 1, F_W, V_F), lambda t, *_: (0, t, 0, 0))
    else:
        x_spec = pl.BlockSpec((1, F_W, VERT), lambda t, *_: (t, 0, 0))
    return pl.pallas_call(
        functools.partial(spread_kernel, chunked),
        grid_spec=pltpu.PrefetchScalarGridSpec(
            num_scalar_prefetch=3,
            grid=(2,),
            in_specs=[
                x_spec,
                pl.BlockSpec((1, MAXT, TILE, TILE), lambda t, *_: (t, 0, 0, 0)),
            ],
            out_specs=pl.BlockSpec((F_DEV, 1, F_W, V_F), lambda t, *_: (0, t, 0, 0)),
            scratch_shapes=[pltpu.VMEM((BLOCKS + 1, F_W, TILE), f32)],
        ),
        out_shape=jax.ShapeDtypeStruct((F_DEV, 2, F_W, V_F), bf16),
        compiler_params=params(24),
        name="spread",
    )(counts, rows, cols, x, tiles)


def mixed(s_ref, x_ref, w_ref):
    m = jnp.dot(w_ref[...].T, s_ref[...].reshape(D, V_F), preferred_element_type=f32)
    h = x_ref[...].reshape(D, V_F).astype(f32) + jnp.maximum(m, 0.0)
    return h.astype(bf16)


def mix_one_kernel(s_ref, x_ref, w_ref, out_ref):
    out_ref[...] = mixed(s_ref, x_ref, w_ref).reshape(F_DEV, 1, F_W, V_F)


def mix_two_kernel(s_ref, x_ref, w_ref, out_ref):
    out_ref[...] = mixed(s_ref, x_ref, w_ref).T.reshape(S_DEV, V_S, D)


def mix(s, x, w, last):
    chunk = pl.BlockSpec((F_DEV, 1, F_W, V_F), lambda t: (0, t, 0, 0))
    if last:
        out_spec = pl.BlockSpec((S_DEV, V_S, D), lambda t: (0, t, 0))
        out_shape = jax.ShapeDtypeStruct((S_DEV, 2 * V_S, D), bf16)
    else:
        out_spec = chunk
        out_shape = jax.ShapeDtypeStruct((F_DEV, 2, F_W, V_F), bf16)
    return pl.pallas_call(
        mix_two_kernel if last else mix_one_kernel,
        grid=(2,),
        in_specs=[chunk, chunk, pl.BlockSpec((D, D), lambda t: (0, 0))],
        out_specs=out_spec,
        out_shape=out_shape,
        compiler_params=params(24),
        name="mix",
    )(s, x, w)


def attend_kernel(h_ref, wq_ref, wk_ref, wv_ref, wo_ref, out_ref, hs, es, wqt, wvt):
    rows = SNAPS * V_S
    for k in range(2):
        hs[k] = h_ref[:, :, k * 128 : (k + 1) * 128].reshape(rows, 128).astype(f32)
    wqt[...] = wq_ref[...].T
    wvt[...] = wv_ref[...].T
    causal = lax.broadcasted_iota(jnp.int32, (SNAPS, SNAPS), 0) <= lax.broadcasted_iota(
        jnp.int32, (SNAPS, SNAPS), 1
    )
    scale = HEAD_DIM**-0.5

    def vertex(v, _):
        hv = jnp.concatenate([hs[k, pl.ds(v, SNAPS, stride=V_S), :] for k in range(2)], axis=1)
        hb = hv.astype(bf16)
        q_t = lax.dot_general(wqt[...], hb, NT, preferred_element_type=f32).astype(bf16)
        v_t = lax.dot_general(wvt[...], hb, NT, preferred_element_type=f32).astype(bf16)
        key = jnp.dot(hb, wk_ref[...], preferred_element_type=f32).astype(bf16)

        def padded(h):
            parts = [q_t[h * HEAD_DIM : (h + 1) * HEAD_DIM]]
            if h > 0:
                parts.insert(0, jnp.zeros((h * HEAD_DIM, SNAPS), bf16))
            if h < HEADS - 1:
                parts.append(jnp.zeros((D - (h + 1) * HEAD_DIM, SNAPS), bf16))
            return jnp.concatenate(parts, axis=0)

        context = []
        for pair in range(HEADS // 2):
            q_pair = jnp.concatenate([padded(2 * pair), padded(2 * pair + 1)], axis=1)
            scores = jnp.dot(key, q_pair, preferred_element_type=f32)
            for k in range(2):
                h = 2 * pair + k
                s = jnp.where(causal, scores[:, k * SNAPS : (k + 1) * SNAPS], masked_score)
                top = jnp.max(s, axis=0, keepdims=True)
                lifted = jnp.exp((s - top) * scale)
                total = jnp.sum(lifted, axis=0, keepdims=True)
                weights = (lifted * (1.0 / total)).astype(bf16)
                context.append(
                    jnp.dot(
                        v_t[h * HEAD_DIM : (h + 1) * HEAD_DIM],
                        weights,
                        preferred_element_type=f32,
                    ).astype(bf16)
                )
        context = jnp.concatenate(context, axis=0).T
        evolved = hv + jnp.dot(context, wo_ref[...], preferred_element_type=f32)
        for k in range(2):
            es[k, pl.ds(v, SNAPS, stride=V_S), :] = evolved[:, k * 128 : (k + 1) * 128]
        return 0

    lax.fori_loop(0, V_S, vertex, 0)
    low = lax.broadcasted_iota(jnp.int32, (V_S, 128), 1) < F_W

    def pack(s, _):
        for k in range(2):
            base = pl.multiple_of(s * 2 * V_S, 2 * V_S)
            even = es[k, pl.ds(base, V_S), :]
            odd = es[k, pl.ds(base + V_S, V_S), :]
            out_ref[2 * k, s] = jnp.where(low, even, pltpu.roll(odd, F_W, 1)).astype(bf16)
            out_ref[2 * k + 1, s] = jnp.where(low, pltpu.roll(even, F_W, 1), odd).astype(bf16)
        return 0

    lax.fori_loop(0, S_DEV, pack, 0, unroll=4)


def attend(hidden, wq, wk, wv, wo):
    rows = SNAPS * V_S
    return pl.pallas_call(
        attend_kernel,
        out_shape=jax.ShapeDtypeStruct((F_DEV, S_DEV, V_S, 2 * F_W), bf16),
        scratch_shapes=[
            pltpu.VMEM((2, rows, 128), f32),
            pltpu.VMEM((2, rows, 128), f32),
            pltpu.VMEM((D, D), bf16),
            pltpu.VMEM((D, D), bf16),
        ],
        compiler_params=params(32),
        name="attend",
    )(hidden, wq, wk, wv, wo)


def place_kernel(in_ref, out_ref):
    for g in range(8):
        block = in_ref[g * 8 : (g + 1) * 8].reshape(128, 128).T
        out_ref[0, :, g * 128 : (g + 1) * 128] = block[:F_W]
        out_ref[1, :, g * 128 : (g + 1) * 128] = block[F_W:]


def place(pieces):
    return pl.pallas_call(
        place_kernel,
        grid=(4,),
        in_specs=[pl.BlockSpec((S_DEV, V_S, 2 * F_W), lambda g: (g, 0, 0))],
        out_specs=pl.BlockSpec((2, F_W, V_F), lambda g: (0, 0, g)),
        out_shape=jax.ShapeDtypeStruct((2, F_W, VERT), bf16),
        compiler_params=params(24),
        name="place",
    )(pieces)


def on_device(
    node_features,
    tile_rows,
    tile_cols,
    tile_counts,
    tile_values,
    layer_one,
    layer_two,
    query_weight,
    key_weight,
    value_weight,
    out_weight,
):
    x = jnp.swapaxes(node_features, 1, 2)

    def turn(a):
        return lax.all_to_all(a, "feat", split_axis=0, concat_axis=0, tiled=True)

    x_rows = turn(jnp.moveaxis(x.reshape(2, F_W, F_DEV, V_F), 2, 0))
    s_one = spread(x, tile_values, tile_rows, tile_cols, tile_counts, False)
    hidden_one = mix(turn(s_one), x_rows, layer_one, False)
    s_two = spread(turn(hidden_one), tile_values, tile_rows, tile_cols, tile_counts, True)
    hidden_two = mix(turn(s_two), hidden_one, layer_two, True)
    owned = lax.all_to_all(hidden_two, "snap", split_axis=0, concat_axis=0, tiled=True)
    evolved = attend(owned, query_weight, key_weight, value_weight, out_weight)
    pieces = lax.all_to_all(
        evolved.reshape(F_DEV * S_DEV, V_S, 2 * F_W),
        ("feat", "snap"),
        split_axis=0,
        concat_axis=0,
        tiled=True,
    )
    return jnp.swapaxes(place(pieces), 1, 2)


def solution(mesh):
    placed = (
        P("snap", None, "feat"),
        P("snap", None),
        P("snap", None),
        P("snap"),
        P("snap", None, None, None),
        P(),
        P(),
        P(),
        P(),
        P(),
        P(),
    )
    return jax.shard_map(
        on_device, mesh=mesh, in_specs=placed, out_specs=P("snap", None, "feat"), check_vma=False
    )
```

```python
import functools

import jax
import jax.numpy as jnp
from jax import lax
from jax.experimental import pallas as pl
from jax.experimental.pallas import tpu as pltpu
from jax.sharding import PartitionSpec as P

HEADS = 8
HEAD_DIM = 32
TILE = 128
D = 256
SNAPS = 128
VERT = 4096
BLOCKS = 32
MAXT = 64
F_DEV = 4
S_DEV = 64
F_W = D // F_DEV
V_F = VERT // F_DEV
V_S = V_F // S_DEV
GROUP = 8

masked_score = -1e30
f32 = jnp.float32
bf16 = jnp.bfloat16
NT = (((1,), (1,)), ((), ()))
MIB = 2**20


def params(mib):
    return pltpu.CompilerParams(vmem_limit_bytes=mib * MIB)


def cut_kernel(me, *refs):
    for k in range(F_DEV):
        refs[F_DEV + k][...] = refs[k][...]


def cut(me, x):
    def block(k):
        return pl.BlockSpec((2, F_W, V_F), lambda i, me: (0, 0, (me[0] + k) % F_DEV))

    return pl.pallas_call(
        cut_kernel,
        grid_spec=pltpu.PrefetchScalarGridSpec(
            num_scalar_prefetch=1,
            grid=(1,),
            in_specs=[block(k) for k in range(F_DEV)],
            out_specs=[pl.BlockSpec((2, F_W, V_F), lambda i, me: (0, 0, 0))] * F_DEV,
        ),
        out_shape=[CHUNK] * F_DEV,
        compiler_params=params(48),
        name="cut",
    )(me, *([x] * F_DEV))


def turn(blocks):
    return [blocks[0]] + [
        lax.ppermute(blocks[k], "feat", [(i, (i + k) % F_DEV) for i in range(F_DEV)])
        for k in (2, 1, 3)
    ]


def unturned(blocks):
    own, two, one, three = blocks
    return [own, one, two, three]


def spread_kernel(chunked, me_ref, counts, rows, cols, *refs):
    me = me_ref[0]
    if chunked:
        x_refs, (tiles_ref, *out_refs), (acc, xs) = refs[:F_DEV], refs[F_DEV : 2 * F_DEV + 1], refs[-2:]
        for k in range(F_DEV):
            xs[(me + F_DEV - k) % F_DEV] = x_refs[k][0]
    else:
        x_ref, tiles_ref, *out_refs, acc = refs
    t = pl.program_id(0)
    acc[...] = jnp.zeros_like(acc)
    n = counts[t]

    def group(g, _):
        products = []
        for j in range(GROUP):
            i = g * GROUP + j
            col = cols[t, i]
            if chunked:
                x = xs[col // 8, :, pl.ds(pl.multiple_of((col % 8) * TILE, TILE), TILE)]
            else:
                x = x_ref[0, :, pl.ds(pl.multiple_of(col * TILE, TILE), TILE)]
            products.append(
                lax.dot_general(x, tiles_ref[0, i], NT, preferred_element_type=f32)
            )
        for j in range(GROUP):
            i = g * GROUP + j
            row = jnp.where(i < n, rows[t, i], BLOCKS)
            acc[row] += products[j]
        return 0

    lax.fori_loop(0, (n + GROUP - 1) // GROUP, group, 0)
    for k in range(F_DEV):
        first = ((me + k) % F_DEV) * 8
        for b in range(8):
            out_refs[k][0, :, b * TILE : (b + 1) * TILE] = acc[first + b].astype(bf16)


CHUNK = jax.ShapeDtypeStruct((2, F_W, V_F), bf16)


def chunk_spec():
    return pl.BlockSpec((1, F_W, V_F), lambda t, *_: (t, 0, 0))


def spread(me, xs, tiles, rows, cols, counts):
    chunked = len(xs) > 1
    scratch = [pltpu.VMEM((BLOCKS + 1, F_W, TILE), f32)]
    if chunked:
        x_specs = [chunk_spec()] * F_DEV
        scratch.append(pltpu.VMEM((F_DEV, F_W, V_F), bf16))
    else:
        x_specs = [pl.BlockSpec((1, F_W, VERT), lambda t, *_: (t, 0, 0))]
    return pl.pallas_call(
        functools.partial(spread_kernel, chunked),
        grid_spec=pltpu.PrefetchScalarGridSpec(
            num_scalar_prefetch=4,
            grid=(2,),
            in_specs=x_specs
            + [pl.BlockSpec((1, MAXT, TILE, TILE), lambda t, *_: (t, 0, 0, 0))],
            out_specs=[chunk_spec()] * F_DEV,
            scratch_shapes=scratch,
        ),
        out_shape=[CHUNK] * F_DEV,
        compiler_params=params(SPREAD_MIB[chunked]),
        name="spread",
    )(me, counts, rows, cols, *xs, tiles)


SPREAD_MIB = (56, 24)


def relu_mix(me, s_refs, w_ref):
    weight = jnp.concatenate(
        [
            w_ref[pl.ds(pl.multiple_of(((me + F_DEV - k) % F_DEV) * F_W, F_W), F_W), :]
            for k in range(F_DEV)
        ],
        axis=0,
    )
    s = jnp.concatenate([r[0] for r in s_refs], axis=0)
    return jnp.maximum(jnp.dot(weight.T, s, preferred_element_type=f32), 0.0)


def mix_one_kernel(me_ref, *refs):
    me = me_ref[0]
    s_refs, x_refs, w_ref, whole_ref, out_refs = refs[:4], refs[4:8], refs[8], refs[9], refs[10:]
    for k in range(F_DEV):
        start = pl.multiple_of(((me + F_DEV - k) % F_DEV) * F_W, F_W)
        whole_ref[0, pl.ds(start, F_W), :] = x_refs[k][0]
    whole_ref[0] = (whole_ref[0].astype(f32) + relu_mix(me, s_refs, w_ref)).astype(bf16)
    for k in range(F_DEV):
        start = pl.multiple_of(((me + k) % F_DEV) * F_W, F_W)
        out_refs[k][0] = whole_ref[0, pl.ds(start, F_W), :]


def mix_two_kernel(me_ref, *refs):
    me = me_ref[0]
    s_refs, h_ref, w_ref, out_ref = refs[:4], refs[4], refs[5], refs[6]
    h = (h_ref[0].astype(f32) + relu_mix(me, s_refs, w_ref)).astype(bf16)
    out_ref[...] = h.T.reshape(S_DEV, V_S, D)


def mix_one(me, s, x, w):
    whole = pl.BlockSpec((1, D, V_F), lambda t, *_: (t, 0, 0))
    first, *rest = pl.pallas_call(
        mix_one_kernel,
        grid_spec=pltpu.PrefetchScalarGridSpec(
            num_scalar_prefetch=1,
            grid=(2,),
            in_specs=[chunk_spec()] * 8 + [pl.BlockSpec((D, D), lambda t, *_: (0, 0))],
            out_specs=[whole] + [chunk_spec()] * F_DEV,
        ),
        out_shape=[jax.ShapeDtypeStruct((2, D, V_F), bf16)] + [CHUNK] * F_DEV,
        compiler_params=params(24),
        name="mix_one",
    )(me, *s, *x, w)
    return first, rest


def mix_two(me, s, h, w):
    return pl.pallas_call(
        mix_two_kernel,
        grid_spec=pltpu.PrefetchScalarGridSpec(
            num_scalar_prefetch=1,
            grid=(2,),
            in_specs=[chunk_spec()] * F_DEV
            + [
                pl.BlockSpec((1, D, V_F), lambda t, *_: (t, 0, 0)),
                pl.BlockSpec((D, D), lambda t, *_: (0, 0)),
            ],
            out_specs=pl.BlockSpec((S_DEV, V_S, D), lambda t, *_: (0, t, 0)),
        ),
        out_shape=jax.ShapeDtypeStruct((S_DEV, 2 * V_S, D), bf16),
        compiler_params=params(24),
        name="mix_two",
    )(me, *s, h, w)


def attend_kernel(h_ref, wq_ref, wk_ref, wv_ref, wo_ref, out_ref, hs, es, hb, qt, vt, ks, ct):
    rows = SNAPS * V_S
    for k in range(2):
        hs[k] = h_ref[:, :, k * 128 : (k + 1) * 128].reshape(rows, 128).astype(f32)
    for v in range(V_S):
        for k in range(2):
            hb[v * SNAPS : (v + 1) * SNAPS, k * 128 : (k + 1) * 128] = hs[
                k, pl.ds(v, SNAPS, stride=V_S), :
            ].astype(bf16)
    wqt = wq_ref[...].T
    wvt = wv_ref[...].T

    def project(c, _):
        at = pl.ds(pl.multiple_of(c * 512, 512), 512)
        x = hb[at, :]
        qt[:, at] = lax.dot_general(wqt, x, NT, preferred_element_type=f32).astype(bf16)
        vt[:, at] = lax.dot_general(wvt, x, NT, preferred_element_type=f32).astype(bf16)
        ks[at, :] = jnp.dot(x, wk_ref[...], preferred_element_type=f32).astype(bf16)
        return 0

    lax.fori_loop(0, rows // 512, project, 0)
    causal = lax.broadcasted_iota(jnp.int32, (SNAPS, SNAPS), 0) <= lax.broadcasted_iota(
        jnp.int32, (SNAPS, SNAPS), 1
    )
    scale = HEAD_DIM**-0.5

    def vertex(v, _):
        at = pl.ds(pl.multiple_of(v * SNAPS, SNAPS), SNAPS)
        key = ks[at, :]

        def padded(h):
            parts = [qt[h * HEAD_DIM : (h + 1) * HEAD_DIM, at]]
            if h > 0:
                parts.insert(0, jnp.zeros((h * HEAD_DIM, SNAPS), bf16))
            if h < HEADS - 1:
                parts.append(jnp.zeros((D - (h + 1) * HEAD_DIM, SNAPS), bf16))
            return jnp.concatenate(parts, axis=0)

        for pair in range(HEADS // 2):
            q_pair = jnp.concatenate([padded(2 * pair), padded(2 * pair + 1)], axis=1)
            scores = jnp.dot(key, q_pair, preferred_element_type=f32)
            for k in range(2):
                head = slice((2 * pair + k) * HEAD_DIM, (2 * pair + k + 1) * HEAD_DIM)
                s = jnp.where(causal, scores[:, k * SNAPS : (k + 1) * SNAPS], masked_score)
                top = jnp.max(s, axis=0, keepdims=True)
                lifted = jnp.exp((s - top) * scale)
                total = jnp.sum(lifted, axis=0, keepdims=True)
                weights = (lifted * (1.0 / total)).astype(bf16)
                ct[head, at] = jnp.dot(
                    vt[head, at], weights, preferred_element_type=f32
                ).astype(bf16)
        return 0

    lax.fori_loop(0, V_S, vertex, 0, unroll=2)
    for v in range(V_S):
        mixed = jnp.dot(
            ct[:, v * SNAPS : (v + 1) * SNAPS].T, wo_ref[...], preferred_element_type=f32
        )
        for k in range(2):
            at = pl.ds(v, SNAPS, stride=V_S)
            es[k, at, :] = hs[k, at, :] + mixed[:, k * 128 : (k + 1) * 128]
    low = lax.broadcasted_iota(jnp.int32, (V_S, 128), 1) < F_W

    def pack(s, _):
        for k in range(2):
            base = pl.multiple_of(s * 2 * V_S, 2 * V_S)
            even = es[k, pl.ds(base, V_S), :]
            odd = es[k, pl.ds(base + V_S, V_S), :]
            out_ref[2 * k, s] = jnp.where(low, even, pltpu.roll(odd, F_W, 1)).astype(bf16)
            out_ref[2 * k + 1, s] = jnp.where(low, pltpu.roll(even, F_W, 1), odd).astype(bf16)
        return 0

    lax.fori_loop(0, S_DEV, pack, 0, unroll=4)


def attend(hidden, wq, wk, wv, wo):
    rows = SNAPS * V_S
    return pl.pallas_call(
        attend_kernel,
        out_shape=jax.ShapeDtypeStruct((F_DEV, S_DEV, V_S, 2 * F_W), bf16),
        scratch_shapes=[
            pltpu.VMEM((2, rows, 128), f32),
            pltpu.VMEM((2, rows, 128), f32),
            pltpu.VMEM((rows, D), bf16),
            pltpu.VMEM((D, rows), bf16),
            pltpu.VMEM((D, rows), bf16),
            pltpu.VMEM((rows, D), bf16),
            pltpu.VMEM((D, rows), bf16),
        ],
        compiler_params=params(32),
        name="attend",
    )(hidden, wq, wk, wv, wo)


def place_kernel(in_ref, out_ref):
    for g in range(8):
        block = in_ref[g * 8 : (g + 1) * 8].reshape(128, 128).T
        out_ref[0, :, g * 128 : (g + 1) * 128] = block[:F_W]
        out_ref[1, :, g * 128 : (g + 1) * 128] = block[F_W:]


def place(pieces):
    return pl.pallas_call(
        place_kernel,
        grid=(4,),
        in_specs=[pl.BlockSpec((S_DEV, V_S, 2 * F_W), lambda g: (g, 0, 0))],
        out_specs=pl.BlockSpec((2, F_W, V_F), lambda g: (0, 0, g)),
        out_shape=jax.ShapeDtypeStruct((2, F_W, VERT), bf16),
        compiler_params=params(24),
        name="place",
    )(pieces)


def on_device(
    node_features,
    tile_rows,
    tile_cols,
    tile_counts,
    tile_values,
    layer_one,
    layer_two,
    query_weight,
    key_weight,
    value_weight,
    out_weight,
):
    x = jnp.swapaxes(node_features, 1, 2)
    me = lax.axis_index("feat").astype(jnp.int32).reshape(1)
    lists = (tile_values, tile_rows, tile_cols, tile_counts)

    x_rows = unturned(turn(cut(me, x)))
    s_one = unturned(turn(spread(me, [x], *lists)))
    hidden_one, h_cut = mix_one(me, s_one, x_rows, layer_one)
    s_two = unturned(turn(spread(me, unturned(turn(h_cut)), *lists)))
    hidden_two = mix_two(me, s_two, hidden_one, layer_two)
    owned = lax.all_to_all(hidden_two, "snap", split_axis=0, concat_axis=0, tiled=True)
    evolved = attend(owned, query_weight, key_weight, value_weight, out_weight)
    pieces = lax.all_to_all(
        evolved.reshape(F_DEV * S_DEV, V_S, 2 * F_W),
        ("feat", "snap"),
        split_axis=0,
        concat_axis=0,
        tiled=True,
    )
    return jnp.swapaxes(place(pieces), 1, 2)


def solution(mesh):
    placed = (
        P("snap", None, "feat"),
        P("snap", None),
        P("snap", None),
        P("snap"),
        P("snap", None, None, None),
        P(),
        P(),
        P(),
        P(),
        P(),
        P(),
    )
    return jax.shard_map(
        on_device, mesh=mesh, in_specs=placed, out_specs=P("snap", None, "feat"), check_vma=False
    )
```

```python
import functools

import jax
import jax.numpy as jnp
from jax import lax
from jax.experimental import pallas as pl
from jax.experimental.pallas import tpu as pltpu
from jax.sharding import PartitionSpec as P

HEADS = 8
HEAD_DIM = 32
TILE = 128
D = 256
SNAPS = 128
VERT = 4096
BLOCKS = 32
MAXT = 64
F_DEV = 4
S_DEV = 64
F_W = D // F_DEV
V_F = VERT // F_DEV
V_S = V_F // S_DEV
GROUP = 8

masked_score = -1e30
f32 = jnp.float32
bf16 = jnp.bfloat16
NT = (((1,), (1,)), ((), ()))
MIB = 2**20


def params(mib):
    return pltpu.CompilerParams(vmem_limit_bytes=mib * MIB)


GROUPS = MAXT // GROUP
SMEM = pl.BlockSpec(memory_space=pltpu.SMEM)
HBM = pl.BlockSpec(memory_space=pl.ANY)
VMEM = pl.BlockSpec(memory_space=pltpu.VMEM)
CHUNK = jax.ShapeDtypeStruct((F_W, V_F), bf16)
PAIR = jax.ShapeDtypeStruct((2, F_W, V_F), bf16)


def cost(us):
    return pl.CostEstimate(flops=int(us * 1e9), bytes_accessed=2**20, transcendentals=0)


def turn(blocks):
    sent = {
        k: lax.ppermute(blocks[k], "feat", [(i, (i + k) % F_DEV) for i in range(F_DEV)])
        for k in (2, 1, 3)
    }
    return [blocks[0], sent[1], sent[2], sent[3]]


def add_tiles(t, counts, rows, cols, features, tiles, acc, ready):
    n = counts[t]
    acc[...] = jnp.zeros_like(acc)

    def group(g, _):
        ready(g)
        products = []
        for j in range(GROUP):
            i = g * GROUP + j
            products.append(
                lax.dot_general(features(cols[t, i]), tiles(i), NT, preferred_element_type=f32)
            )
        for j in range(GROUP):
            i = g * GROUP + j
            row = jnp.where(i < n, rows[t, i], BLOCKS)
            acc[row] += products[j]
        return 0

    lax.fori_loop(0, (n + GROUP - 1) // GROUP, group, 0)


def spread_one_kernel(t, me_ref, counts, rows, cols, x_hbm, tiles_hbm, *refs):
    out_refs, (acc, x, tiles, x_sem, sems) = refs[:F_DEV], refs[F_DEV:]
    me = me_ref[0]
    fetch_x = pltpu.make_async_copy(x_hbm.at[t], x, x_sem)
    fetch_x.start()

    def fetch(g):
        at = pl.ds(g * GROUP, GROUP)
        return pltpu.make_async_copy(tiles_hbm.at[t, at], tiles.at[at], sems.at[g])

    def start(g, _):
        fetch(g).start()
        return 0

    lax.fori_loop(0, (counts[t] + GROUP - 1) // GROUP, start, 0)
    fetch_x.wait()
    add_tiles(
        t,
        counts,
        rows,
        cols,
        lambda col: x[:, pl.ds(pl.multiple_of(col * TILE, TILE), TILE)],
        lambda i: tiles[i],
        acc,
        lambda g: fetch(g).wait(),
    )
    for k in range(F_DEV):
        block = (me + k) % F_DEV
        out_refs[k][0] = x[:, pl.ds(pl.multiple_of(block * V_F, V_F), V_F)]
        for b in range(8):
            out_refs[k][1, :, b * TILE : (b + 1) * TILE] = acc[block * 8 + b].astype(bf16)


def spread_one(t, me, x, tiles, rows, cols, counts):
    return pl.pallas_call(
        functools.partial(spread_one_kernel, t),
        in_specs=[SMEM] * 4 + [HBM] * 2,
        out_specs=[VMEM] * F_DEV,
        out_shape=[PAIR] * F_DEV,
        scratch_shapes=[
            pltpu.VMEM((BLOCKS + 1, F_W, TILE), f32),
            pltpu.VMEM((F_W, VERT), bf16),
            pltpu.VMEM((MAXT, TILE, TILE), bf16),
            pltpu.SemaphoreType.DMA,
            pltpu.SemaphoreType.DMA((GROUPS,)),
        ],
        compiler_params=params(SPREAD_MIB),
        cost_estimate=cost(4),
        name="spread_one",
    )(me, counts, rows, cols, x, tiles)


SPREAD_MIB = 56


def spread_two_kernel(t, me_ref, counts, rows, cols, *refs):
    h_refs, tiles, out_refs, (acc, h) = refs[:4], refs[4], refs[5:9], refs[9:]
    me = me_ref[0]
    for k in range(F_DEV):
        h[(me + F_DEV - k) % F_DEV] = h_refs[k][...]
    add_tiles(
        t,
        counts,
        rows,
        cols,
        lambda col: h[col // 8, :, pl.ds(pl.multiple_of((col % 8) * TILE, TILE), TILE)],
        lambda i: tiles[0, i],
        acc,
        lambda g: None,
    )
    for k in range(F_DEV):
        block = (me + k) % F_DEV
        for b in range(8):
            out_refs[k][:, b * TILE : (b + 1) * TILE] = acc[block * 8 + b].astype(bf16)


def spread_two(t, me, h, tiles, rows, cols, counts):
    def full(dims):
        return pl.BlockSpec(dims, lambda i: (0,) * len(dims))

    return pl.pallas_call(
        functools.partial(spread_two_kernel, t),
        grid=(1,),
        in_specs=[SMEM] * 4
        + [full((F_W, V_F))] * F_DEV
        + [pl.BlockSpec((1, MAXT, TILE, TILE), lambda i: (t, 0, 0, 0))],
        out_specs=[full((F_W, V_F))] * F_DEV,
        out_shape=[CHUNK] * F_DEV,
        scratch_shapes=[
            pltpu.VMEM((BLOCKS + 1, F_W, TILE), f32),
            pltpu.VMEM((F_DEV, F_W, V_F), bf16),
        ],
        compiler_params=params(20),
        cost_estimate=cost(3),
        name="spread_two",
    )(me, counts, rows, cols, *h, tiles)


def relu_mix(me, parts, w_ref):
    weight = jnp.concatenate(
        [
            w_ref[pl.ds(pl.multiple_of(((me + F_DEV - k) % F_DEV) * F_W, F_W), F_W), :]
            for k in range(F_DEV)
        ],
        axis=0,
    )
    s = jnp.concatenate(parts, axis=0)
    return jnp.maximum(jnp.dot(weight.T, s, preferred_element_type=f32), 0.0)


def mix_one_kernel(me_ref, *refs):
    me = me_ref[0]
    in_refs, w_ref, whole_ref, out_refs = refs[:4], refs[4], refs[5], refs[6:]
    for k in range(F_DEV):
        start = pl.multiple_of(((me + F_DEV - k) % F_DEV) * F_W, F_W)
        whole_ref[pl.ds(start, F_W), :] = in_refs[k][0]
    mixed = relu_mix(me, [r[1] for r in in_refs], w_ref)
    whole_ref[...] = (whole_ref[...].astype(f32) + mixed).astype(bf16)
    for k in range(F_DEV):
        start = pl.multiple_of(((me + k) % F_DEV) * F_W, F_W)
        out_refs[k][...] = whole_ref[pl.ds(start, F_W), :]


def mix_one(me, parts, w):
    first, *rest = pl.pallas_call(
        mix_one_kernel,
        in_specs=[SMEM] + [VMEM] * 5,
        out_specs=[VMEM] * 5,
        out_shape=[jax.ShapeDtypeStruct((D, V_F), bf16)] + [CHUNK] * F_DEV,
        compiler_params=params(16),
        cost_estimate=cost(1),
        name="mix_one",
    )(me, *parts, w)
    return first, rest


def mix_two_kernel(last, me_ref, *refs):
    me = me_ref[0]
    s_refs, h_ref, w_ref, out_ref = refs[:4], refs[4], refs[5], refs[-1]
    mixed = relu_mix(me, [r[...] for r in s_refs], w_ref)
    h = (h_ref[...].astype(f32) + mixed).astype(bf16).T.reshape(S_DEV, V_S, D)
    if last:
        out_ref[:, :V_S, :] = refs[6][...]
        out_ref[:, V_S:, :] = h
    else:
        out_ref[...] = h


def mix_two(me, s, h, w, before):
    last = len(before)
    return pl.pallas_call(
        functools.partial(mix_two_kernel, last),
        in_specs=[SMEM] + [VMEM] * (6 + last),
        out_specs=VMEM,
        out_shape=jax.ShapeDtypeStruct((S_DEV, V_S * (1 + last), D), bf16),
        compiler_params=params(16),
        cost_estimate=cost(1),
        name="mix_two",
    )(me, *s, h, w, *before)


def attend_kernel(h_ref, wq_ref, wk_ref, wv_ref, wo_ref, out_ref, hs, es, hb, qt, vt, ks, ct):
    rows = SNAPS * V_S
    for k in range(2):
        hs[k] = h_ref[:, :, k * 128 : (k + 1) * 128].reshape(rows, 128).astype(f32)
    for v in range(V_S):
        for k in range(2):
            hb[v * SNAPS : (v + 1) * SNAPS, k * 128 : (k + 1) * 128] = hs[
                k, pl.ds(v, SNAPS, stride=V_S), :
            ].astype(bf16)
    wqt = wq_ref[...].T
    wvt = wv_ref[...].T

    def project(c, _):
        at = pl.ds(pl.multiple_of(c * 512, 512), 512)
        x = hb[at, :]
        qt[:, at] = lax.dot_general(wqt, x, NT, preferred_element_type=f32).astype(bf16)
        vt[:, at] = lax.dot_general(wvt, x, NT, preferred_element_type=f32).astype(bf16)
        ks[at, :] = jnp.dot(x, wk_ref[...], preferred_element_type=f32).astype(bf16)
        return 0

    lax.fori_loop(0, rows // 512, project, 0)
    causal = lax.broadcasted_iota(jnp.int32, (SNAPS, SNAPS), 0) <= lax.broadcasted_iota(
        jnp.int32, (SNAPS, SNAPS), 1
    )
    scale = HEAD_DIM**-0.5

    def vertex(v, _):
        at = pl.ds(pl.multiple_of(v * SNAPS, SNAPS), SNAPS)
        key = ks[at, :]

        def padded(h):
            parts = [qt[h * HEAD_DIM : (h + 1) * HEAD_DIM, at]]
            if h > 0:
                parts.insert(0, jnp.zeros((h * HEAD_DIM, SNAPS), bf16))
            if h < HEADS - 1:
                parts.append(jnp.zeros((D - (h + 1) * HEAD_DIM, SNAPS), bf16))
            return jnp.concatenate(parts, axis=0)

        for pair in range(HEADS // 2):
            q_pair = jnp.concatenate([padded(2 * pair), padded(2 * pair + 1)], axis=1)
            scores = jnp.dot(key, q_pair, preferred_element_type=f32)
            for k in range(2):
                head = slice((2 * pair + k) * HEAD_DIM, (2 * pair + k + 1) * HEAD_DIM)
                s = jnp.where(causal, scores[:, k * SNAPS : (k + 1) * SNAPS], masked_score)
                top = jnp.max(s, axis=0, keepdims=True)
                lifted = jnp.exp((s - top) * scale)
                total = jnp.sum(lifted, axis=0, keepdims=True)
                weights = (lifted * (1.0 / total)).astype(bf16)
                ct[head, at] = jnp.dot(
                    vt[head, at], weights, preferred_element_type=f32
                ).astype(bf16)
        return 0

    lax.fori_loop(0, V_S, vertex, 0, unroll=4)
    for v in range(V_S):
        mixed = jnp.dot(
            ct[:, v * SNAPS : (v + 1) * SNAPS].T, wo_ref[...], preferred_element_type=f32
        )
        for k in range(2):
            at = pl.ds(v, SNAPS, stride=V_S)
            es[k, at, :] = hs[k, at, :] + mixed[:, k * 128 : (k + 1) * 128]
    low = lax.broadcasted_iota(jnp.int32, (PACK, V_S, 128), 2) < F_W

    def pack(c, _):
        base = pl.multiple_of(c * PACK * 2 * V_S, PACK * 2 * V_S)
        at = pl.ds(c * PACK, PACK)
        for k in range(2):
            both = es[k, pl.ds(base, PACK * 2 * V_S), :].reshape(PACK, 2, V_S, 128)
            even, odd = both[:, 0], both[:, 1]
            out_ref[2 * k, at] = jnp.where(low, even, pltpu.roll(odd, F_W, 2)).astype(bf16)
            out_ref[2 * k + 1, at] = jnp.where(low, pltpu.roll(even, F_W, 2), odd).astype(bf16)
        return 0

    lax.fori_loop(0, S_DEV // PACK, pack, 0)


PACK = 16


def attend(hidden, wq, wk, wv, wo):
    rows = SNAPS * V_S
    return pl.pallas_call(
        attend_kernel,
        out_shape=jax.ShapeDtypeStruct((F_DEV, S_DEV, V_S, 2 * F_W), bf16),
        scratch_shapes=[
            pltpu.VMEM((2, rows, 128), f32),
            pltpu.VMEM((2, rows, 128), f32),
            pltpu.VMEM((rows, D), bf16),
            pltpu.VMEM((D, rows), bf16),
            pltpu.VMEM((D, rows), bf16),
            pltpu.VMEM((rows, D), bf16),
            pltpu.VMEM((D, rows), bf16),
        ],
        compiler_params=params(32),
        name="attend",
    )(hidden, wq, wk, wv, wo)


def place_kernel(in_ref, out_ref):
    for g in range(8):
        block = in_ref[g * 8 : (g + 1) * 8].reshape(128, 128).T
        out_ref[0, :, g * 128 : (g + 1) * 128] = block[:F_W]
        out_ref[1, :, g * 128 : (g + 1) * 128] = block[F_W:]


def place(pieces):
    return pl.pallas_call(
        place_kernel,
        grid=(4,),
        in_specs=[pl.BlockSpec((S_DEV, V_S, 2 * F_W), lambda g: (g, 0, 0))],
        out_specs=pl.BlockSpec((2, F_W, V_F), lambda g: (0, 0, g)),
        out_shape=jax.ShapeDtypeStruct((2, F_W, VERT), bf16),
        compiler_params=params(24),
        name="place",
    )(pieces)


def on_device(
    node_features,
    tile_rows,
    tile_cols,
    tile_counts,
    tile_values,
    layer_one,
    layer_two,
    query_weight,
    key_weight,
    value_weight,
    out_weight,
):
    x = jnp.swapaxes(node_features, 1, 2)
    me = lax.axis_index("feat").astype(jnp.int32).reshape(1)
    lists = (tile_values, tile_rows, tile_cols, tile_counts)

    both = range(2)
    s_one = [turn(spread_one(t, me, x, *lists)) for t in both]
    ones = [mix_one(me, s_one[t], layer_one) for t in both]
    h_one = [turn(ones[t][1]) for t in both]
    s_two = [turn(spread_two(t, me, h_one[t], *lists)) for t in both]
    hidden = []
    for t in both:
        hidden = [mix_two(me, s_two[t], ones[t][0], layer_two, hidden)]
    owned = lax.all_to_all(hidden[0], "snap", split_axis=0, concat_axis=0, tiled=True)
    evolved = attend(owned, query_weight, key_weight, value_weight, out_weight)
    pieces = lax.all_to_all(
        evolved.reshape(F_DEV * S_DEV, V_S, 2 * F_W),
        ("feat", "snap"),
        split_axis=0,
        concat_axis=0,
        tiled=True,
    )
    return jnp.swapaxes(place(pieces), 1, 2)


def solution(mesh):
    placed = (
        P("snap", None, "feat"),
        P("snap", None),
        P("snap", None),
        P("snap"),
        P("snap", None, None, None),
        P(),
        P(),
        P(),
        P(),
        P(),
        P(),
    )
    return jax.shard_map(
        on_device, mesh=mesh, in_specs=placed, out_specs=P("snap", None, "feat"), check_vma=False
    )
```

```python
import functools

import jax
import jax.numpy as jnp
from jax import lax
from jax.experimental import pallas as pl
from jax.experimental.pallas import tpu as pltpu
from jax.sharding import PartitionSpec as P

HEADS = 8
HEAD_DIM = 32
TILE = 128
D = 256
SNAPS = 128
VERT = 4096
BLOCKS = 32
MAXT = 64
F_DEV = 4
S_DEV = 64
F_W = D // F_DEV
V_F = VERT // F_DEV
V_S = V_F // S_DEV
GROUP = 8

masked_score = -1e30
LOG2_E = 1.4426950408889634
f32 = jnp.float32
bf16 = jnp.bfloat16
NT = (((1,), (1,)), ((), ()))
MIB = 2**20


def params(mib):
    return pltpu.CompilerParams(vmem_limit_bytes=mib * MIB)


GROUPS = MAXT // GROUP
SMEM = pl.BlockSpec(memory_space=pltpu.SMEM)
HBM = pl.BlockSpec(memory_space=pl.ANY)
VMEM = pl.BlockSpec(memory_space=pltpu.VMEM)
CHUNK = jax.ShapeDtypeStruct((F_W, V_F), bf16)
PAIR = jax.ShapeDtypeStruct((2, F_W, V_F), bf16)


def cost(us):
    return pl.CostEstimate(flops=int(us * 1e9), bytes_accessed=2**20, transcendentals=0)


def turn(blocks):
    sent = {
        k: lax.ppermute(blocks[k], "feat", [(i, (i + k) % F_DEV) for i in range(F_DEV)])
        for k in (2, 1, 3)
    }
    return [blocks[0], sent[1], sent[2], sent[3]]


def add_tiles(t, counts, rows, cols, features, tiles, acc, ready):
    n = counts[t]
    acc[...] = jnp.zeros_like(acc)

    def group(g, _):
        ready(g)
        products = []
        for j in range(GROUP):
            i = g * GROUP + j
            products.append(
                lax.dot_general(features(cols[t, i]), tiles(i), NT, preferred_element_type=f32)
            )
        for j in range(GROUP):
            i = g * GROUP + j
            row = jnp.where(i < n, rows[t, i], BLOCKS)
            acc[row] += products[j]
        return 0

    lax.fori_loop(0, (n + GROUP - 1) // GROUP, group, 0)


def spread_one_kernel(t, me_ref, counts, rows, cols, x_hbm, tiles_hbm, *refs):
    out_refs, (acc, x, tiles, x_sem, sems) = refs[:F_DEV], refs[F_DEV:]
    me = me_ref[0]
    fetch_x = pltpu.make_async_copy(x_hbm.at[t], x, x_sem)
    fetch_x.start()

    def fetch(g):
        at = pl.ds(g * GROUP, GROUP)
        return pltpu.make_async_copy(tiles_hbm.at[t, at], tiles.at[at], sems.at[g])

    def start(g, _):
        fetch(g).start()
        return 0

    lax.fori_loop(0, (counts[t] + GROUP - 1) // GROUP, start, 0)
    fetch_x.wait()
    add_tiles(
        t,
        counts,
        rows,
        cols,
        lambda col: x[:, pl.ds(pl.multiple_of(col * TILE, TILE), TILE)],
        lambda i: tiles[i],
        acc,
        lambda g: fetch(g).wait(),
    )
    for k in range(F_DEV):
        block = (me + k) % F_DEV
        out_refs[k][0] = x[:, pl.ds(pl.multiple_of(block * V_F, V_F), V_F)]
        for b in range(8):
            out_refs[k][1, :, b * TILE : (b + 1) * TILE] = acc[block * 8 + b].astype(bf16)


def spread_one(t, me, x, tiles, rows, cols, counts):
    return pl.pallas_call(
        functools.partial(spread_one_kernel, t),
        in_specs=[SMEM] * 4 + [HBM] * 2,
        out_specs=[VMEM] * F_DEV,
        out_shape=[PAIR] * F_DEV,
        scratch_shapes=[
            pltpu.VMEM((BLOCKS + 1, F_W, TILE), f32),
            pltpu.VMEM((F_W, VERT), bf16),
            pltpu.VMEM((MAXT, TILE, TILE), bf16),
            pltpu.SemaphoreType.DMA,
            pltpu.SemaphoreType.DMA((GROUPS,)),
        ],
        compiler_params=params(SPREAD_MIB[t]),
        cost_estimate=cost(4),
        name="spread_one",
    )(me, counts, rows, cols, x, tiles)


SPREAD_MIB = (56, 52)


def spread_two_kernel(t, me_ref, counts, rows, cols, *refs):
    h_refs, tiles, out_refs, (acc, h) = refs[:4], refs[4], refs[5:9], refs[9:]
    me = me_ref[0]
    for k in range(F_DEV):
        h[(me + F_DEV - k) % F_DEV] = h_refs[k][...]
    add_tiles(
        t,
        counts,
        rows,
        cols,
        lambda col: h[col // 8, :, pl.ds(pl.multiple_of((col % 8) * TILE, TILE), TILE)],
        lambda i: tiles[0, i],
        acc,
        lambda g: None,
    )
    for k in range(F_DEV):
        block = (me + k) % F_DEV
        for b in range(8):
            out_refs[k][:, b * TILE : (b + 1) * TILE] = acc[block * 8 + b].astype(bf16)


def spread_two(t, me, h, tiles, rows, cols, counts):
    def full(dims):
        return pl.BlockSpec(dims, lambda i: (0,) * len(dims))

    return pl.pallas_call(
        functools.partial(spread_two_kernel, t),
        grid=(1,),
        in_specs=[SMEM] * 4
        + [full((F_W, V_F))] * F_DEV
        + [pl.BlockSpec((1, MAXT, TILE, TILE), lambda i: (t, 0, 0, 0))],
        out_specs=[full((F_W, V_F))] * F_DEV,
        out_shape=[CHUNK] * F_DEV,
        scratch_shapes=[
            pltpu.VMEM((BLOCKS + 1, F_W, TILE), f32),
            pltpu.VMEM((F_DEV, F_W, V_F), bf16),
        ],
        compiler_params=params(20),
        cost_estimate=cost(3),
        name="spread_two",
    )(me, counts, rows, cols, *h, tiles)


def relu_mix(me, parts, w_ref):
    weight = jnp.concatenate(
        [
            w_ref[pl.ds(pl.multiple_of(((me + F_DEV - k) % F_DEV) * F_W, F_W), F_W), :]
            for k in range(F_DEV)
        ],
        axis=0,
    )
    s = jnp.concatenate(parts, axis=0)
    return jnp.maximum(jnp.dot(weight.T, s, preferred_element_type=f32), 0.0)


def mix_one_kernel(me_ref, *refs):
    me = me_ref[0]
    in_refs, w_ref, whole_ref, out_refs = refs[:4], refs[4], refs[5], refs[6:]
    for k in range(F_DEV):
        start = pl.multiple_of(((me + F_DEV - k) % F_DEV) * F_W, F_W)
        whole_ref[pl.ds(start, F_W), :] = in_refs[k][0]
    mixed = relu_mix(me, [r[1] for r in in_refs], w_ref)
    whole_ref[...] = (whole_ref[...].astype(f32) + mixed).astype(bf16)
    for k in range(F_DEV):
        start = pl.multiple_of(((me + k) % F_DEV) * F_W, F_W)
        out_refs[k][...] = whole_ref[pl.ds(start, F_W), :]


def mix_one(me, parts, w):
    first, *rest = pl.pallas_call(
        mix_one_kernel,
        in_specs=[SMEM] + [VMEM] * 5,
        out_specs=[VMEM] * 5,
        out_shape=[jax.ShapeDtypeStruct((D, V_F), bf16)] + [CHUNK] * F_DEV,
        compiler_params=params(16),
        cost_estimate=cost(1),
        name="mix_one",
    )(me, *parts, w)
    return first, rest


def mix_two_kernel(last, me_ref, *refs):
    me = me_ref[0]
    s_refs, h_ref, w_ref, out_ref = refs[:4], refs[4], refs[5], refs[-1]
    mixed = relu_mix(me, [r[...] for r in s_refs], w_ref)
    h = (h_ref[...].astype(f32) + mixed).astype(bf16).T.reshape(S_DEV, V_S, D)
    if last:
        out_ref[:, :V_S, :] = refs[6][...]
        out_ref[:, V_S:, :] = h
    else:
        out_ref[...] = h


def mix_two(me, s, h, w, before):
    last = len(before)
    return pl.pallas_call(
        functools.partial(mix_two_kernel, last),
        in_specs=[SMEM] + [VMEM] * (6 + last),
        out_specs=VMEM,
        out_shape=jax.ShapeDtypeStruct((S_DEV, V_S * (1 + last), D), bf16),
        compiler_params=params(16),
        cost_estimate=cost(1),
        name="mix_two",
    )(me, *s, h, w, *before)


def attend_kernel(h_ref, wq_ref, wk_ref, wv_ref, wo_ref, out_ref, hs, es, hb, qt, vt, ks, ct):
    rows = SNAPS * V_S
    for k in range(2):
        hs[k] = h_ref[:, :, k * 128 : (k + 1) * 128].reshape(rows, 128).astype(f32)
    for v in range(V_S):
        for k in range(2):
            hb[v * SNAPS : (v + 1) * SNAPS, k * 128 : (k + 1) * 128] = hs[
                k, pl.ds(v, SNAPS, stride=V_S), :
            ].astype(bf16)
    wqt = wq_ref[...].T
    wvt = wv_ref[...].T

    def project(c, _):
        at = pl.ds(pl.multiple_of(c * 512, 512), 512)
        x = hb[at, :]
        qt[:, at] = lax.dot_general(wqt, x, NT, preferred_element_type=f32).astype(bf16)
        vt[:, at] = lax.dot_general(wvt, x, NT, preferred_element_type=f32).astype(bf16)
        ks[at, :] = jnp.dot(x, wk_ref[...], preferred_element_type=f32).astype(bf16)
        return 0

    lax.fori_loop(0, rows // 512, project, 0)
    causal = lax.broadcasted_iota(jnp.int32, (SNAPS, SNAPS), 0) <= lax.broadcasted_iota(
        jnp.int32, (SNAPS, SNAPS), 1
    )
    scale = HEAD_DIM**-0.5 * LOG2_E

    def vertex(v, _):
        at = pl.ds(pl.multiple_of(v * SNAPS, SNAPS), SNAPS)
        key = ks[at, :]

        def padded(h):
            parts = [qt[h * HEAD_DIM : (h + 1) * HEAD_DIM, at]]
            if h > 0:
                parts.insert(0, jnp.zeros((h * HEAD_DIM, SNAPS), bf16))
            if h < HEADS - 1:
                parts.append(jnp.zeros((D - (h + 1) * HEAD_DIM, SNAPS), bf16))
            return jnp.concatenate(parts, axis=0)

        for pair in range(HEADS // 2):
            q_pair = jnp.concatenate([padded(2 * pair), padded(2 * pair + 1)], axis=1)
            scores = jnp.dot(key, q_pair, preferred_element_type=f32)
            for k in range(2):
                head = slice((2 * pair + k) * HEAD_DIM, (2 * pair + k + 1) * HEAD_DIM)
                s = jnp.where(causal, scores[:, k * SNAPS : (k + 1) * SNAPS], masked_score)
                top = jnp.max(s, axis=0, keepdims=True)
                lifted = jnp.exp2((s - top) * scale)
                total = jnp.sum(lifted, axis=0, keepdims=True)
                weights = (lifted * (1.0 / total)).astype(bf16)
                ct[head, at] = jnp.dot(
                    vt[head, at], weights, preferred_element_type=f32
                ).astype(bf16)
        return 0

    lax.fori_loop(0, V_S, vertex, 0, unroll=8)
    for v in range(V_S):
        mixed = jnp.dot(
            ct[:, v * SNAPS : (v + 1) * SNAPS].T, wo_ref[...], preferred_element_type=f32
        )
        for k in range(2):
            at = pl.ds(v, SNAPS, stride=V_S)
            es[k, at, :] = hs[k, at, :] + mixed[:, k * 128 : (k + 1) * 128]
    low = lax.broadcasted_iota(jnp.int32, (PACK, V_S, 128), 2) < F_W

    def pack(c, _):
        base = pl.multiple_of(c * PACK * 2 * V_S, PACK * 2 * V_S)
        at = pl.ds(c * PACK, PACK)
        for k in range(2):
            both = es[k, pl.ds(base, PACK * 2 * V_S), :].reshape(PACK, 2, V_S, 128)
            even, odd = both[:, 0], both[:, 1]
            out_ref[2 * k, at] = jnp.where(low, even, pltpu.roll(odd, F_W, 2)).astype(bf16)
            out_ref[2 * k + 1, at] = jnp.where(low, pltpu.roll(even, F_W, 2), odd).astype(bf16)
        return 0

    lax.fori_loop(0, S_DEV // PACK, pack, 0)


PACK = 16


def attend(hidden, wq, wk, wv, wo):
    rows = SNAPS * V_S
    return pl.pallas_call(
        attend_kernel,
        out_shape=jax.ShapeDtypeStruct((F_DEV, S_DEV, V_S, 2 * F_W), bf16),
        scratch_shapes=[
            pltpu.VMEM((2, rows, 128), f32),
            pltpu.VMEM((2, rows, 128), f32),
            pltpu.VMEM((rows, D), bf16),
            pltpu.VMEM((D, rows), bf16),
            pltpu.VMEM((D, rows), bf16),
            pltpu.VMEM((rows, D), bf16),
            pltpu.VMEM((D, rows), bf16),
        ],
        compiler_params=params(32),
        name="attend",
    )(hidden, wq, wk, wv, wo)


def place_kernel(in_ref, out_ref):
    for g in range(16):
        block = in_ref[g * 8 : (g + 1) * 8].reshape(128, 128).T
        out_ref[0, :, g * 128 : (g + 1) * 128] = block[:F_W]
        out_ref[1, :, g * 128 : (g + 1) * 128] = block[F_W:]


def place(pieces):
    return pl.pallas_call(
        place_kernel,
        grid=(2,),
        in_specs=[pl.BlockSpec((S_DEV * 2, V_S, 2 * F_W), lambda g: (g, 0, 0))],
        out_specs=pl.BlockSpec((2, F_W, V_F * 2), lambda g: (0, 0, g)),
        out_shape=jax.ShapeDtypeStruct((2, F_W, VERT), bf16),
        compiler_params=params(24),
        name="place",
    )(pieces)


def on_device(
    node_features,
    tile_rows,
    tile_cols,
    tile_counts,
    tile_values,
    layer_one,
    layer_two,
    query_weight,
    key_weight,
    value_weight,
    out_weight,
):
    x = jnp.swapaxes(node_features, 1, 2)
    me = lax.axis_index("feat").astype(jnp.int32).reshape(1)
    lists = (tile_values, tile_rows, tile_cols, tile_counts)

    both = range(2)
    s_one = [turn(spread_one(t, me, x, *lists)) for t in both]
    ones = [mix_one(me, s_one[t], layer_one) for t in both]
    h_one = [turn(ones[t][1]) for t in both]
    s_two = [turn(spread_two(t, me, h_one[t], *lists)) for t in both]
    hidden = []
    for t in both:
        hidden = [mix_two(me, s_two[t], ones[t][0], layer_two, hidden)]
    owned = lax.all_to_all(hidden[0], "snap", split_axis=0, concat_axis=0, tiled=True)
    evolved = attend(owned, query_weight, key_weight, value_weight, out_weight)
    pieces = lax.all_to_all(
        evolved.reshape(F_DEV * S_DEV, V_S, 2 * F_W),
        ("feat", "snap"),
        split_axis=0,
        concat_axis=0,
        tiled=True,
    )
    return jnp.swapaxes(place(pieces), 1, 2)


def solution(mesh):
    placed = (
        P("snap", None, "feat"),
        P("snap", None),
        P("snap", None),
        P("snap"),
        P("snap", None, None, None),
        P(),
        P(),
        P(),
        P(),
        P(),
        P(),
    )
    return jax.shard_map(
        on_device, mesh=mesh, in_specs=placed, out_specs=P("snap", None, "feat"), check_vma=False
    )
```

```python
import functools

import jax
import jax.numpy as jnp
from jax import lax
from jax.experimental import pallas as pl
from jax.experimental.pallas import tpu as pltpu
from jax.sharding import PartitionSpec as P

HEADS = 8
HEAD_DIM = 32
TILE = 128
D = 256
SNAPS = 128
VERT = 4096
BLOCKS = 32
MAXT = 64
F_DEV = 4
S_DEV = 64
F_W = D // F_DEV
V_F = VERT // F_DEV
V_S = V_F // S_DEV
GROUP = 8

masked_score = -1e30
LOG2_E = 1.4426950408889634
f32 = jnp.float32
bf16 = jnp.bfloat16
NT = (((1,), (1,)), ((), ()))
MIB = 2**20


def params(mib):
    return pltpu.CompilerParams(vmem_limit_bytes=mib * MIB)


GROUPS = MAXT // GROUP
SMEM = pl.BlockSpec(memory_space=pltpu.SMEM)
HBM = pl.BlockSpec(memory_space=pl.ANY)
VMEM = pl.BlockSpec(memory_space=pltpu.VMEM)
CHUNK = jax.ShapeDtypeStruct((F_W, V_F), bf16)
PAIR = jax.ShapeDtypeStruct((2, F_W, V_F), bf16)


def cost(us):
    return pl.CostEstimate(flops=int(us * 1e9), bytes_accessed=2**20, transcendentals=0)


def turn(blocks):
    sent = {
        k: lax.ppermute(blocks[k], "feat", [(i, (i + k) % F_DEV) for i in range(F_DEV)])
        for k in (2, 1, 3)
    }
    return [blocks[0], sent[1], sent[2], sent[3]]


def add_tiles(t, counts, rows, cols, features, tiles, acc, ready):
    n = counts[t]
    acc[...] = jnp.zeros_like(acc)

    def group(g, _):
        ready(g)
        products = []
        for j in range(GROUP):
            i = g * GROUP + j
            products.append(
                lax.dot_general(features(cols[t, i]), tiles(i), NT, preferred_element_type=f32)
            )
        for j in range(GROUP):
            i = g * GROUP + j
            row = jnp.where(i < n, rows[t, i], BLOCKS)
            acc[row] += products[j]
        return 0

    lax.fori_loop(0, (n + GROUP - 1) // GROUP, group, 0)


def spread_one_kernel(t, me_ref, counts, rows, cols, x_hbm, tiles_hbm, *refs):
    out_refs, (acc, x, tiles, x_sem, sems) = refs[:F_DEV], refs[F_DEV:]
    me = me_ref[0]
    fetch_x = pltpu.make_async_copy(x_hbm.at[t], x, x_sem)
    fetch_x.start()

    def fetch(g):
        at = pl.ds(g * GROUP, GROUP)
        return pltpu.make_async_copy(tiles_hbm.at[t, at], tiles.at[at], sems.at[g])

    def start(g, _):
        fetch(g).start()
        return 0

    lax.fori_loop(0, (counts[t] + GROUP - 1) // GROUP, start, 0)
    fetch_x.wait()
    add_tiles(
        t,
        counts,
        rows,
        cols,
        lambda col: x[:, pl.ds(pl.multiple_of(col * TILE, TILE), TILE)],
        lambda i: tiles[i],
        acc,
        lambda g: fetch(g).wait(),
    )
    for k in range(F_DEV):
        block = (me + k) % F_DEV
        out_refs[k][0] = x[:, pl.ds(pl.multiple_of(block * V_F, V_F), V_F)]
        for b in range(8):
            out_refs[k][1, :, b * TILE : (b + 1) * TILE] = acc[block * 8 + b].astype(bf16)


def spread_one(t, me, x, tiles, rows, cols, counts):
    return pl.pallas_call(
        functools.partial(spread_one_kernel, t),
        in_specs=[SMEM] * 4 + [HBM] * 2,
        out_specs=[VMEM] * F_DEV,
        out_shape=[PAIR] * F_DEV,
        scratch_shapes=[
            pltpu.VMEM((BLOCKS + 1, F_W, TILE), f32),
            pltpu.VMEM((F_W, VERT), bf16),
            pltpu.VMEM((MAXT, TILE, TILE), bf16),
            pltpu.SemaphoreType.DMA,
            pltpu.SemaphoreType.DMA((GROUPS,)),
        ],
        compiler_params=params(SPREAD_MIB[t]),
        cost_estimate=cost(4),
        name="spread_one",
    )(me, counts, rows, cols, x, tiles)


SPREAD_MIB = (56, 52)


def spread_two_kernel(t, me_ref, counts, rows, cols, *refs):
    h_refs, tiles, out_refs, (acc, h) = refs[:4], refs[4], refs[5:9], refs[9:]
    me = me_ref[0]
    for k in range(F_DEV):
        h[(me + F_DEV - k) % F_DEV] = h_refs[k][...]
    add_tiles(
        t,
        counts,
        rows,
        cols,
        lambda col: h[col // 8, :, pl.ds(pl.multiple_of((col % 8) * TILE, TILE), TILE)],
        lambda i: tiles[0, i],
        acc,
        lambda g: None,
    )
    for k in range(F_DEV):
        block = (me + k) % F_DEV
        for b in range(8):
            out_refs[k][:, b * TILE : (b + 1) * TILE] = acc[block * 8 + b].astype(bf16)


def spread_two(t, me, h, tiles, rows, cols, counts):
    def full(dims):
        return pl.BlockSpec(dims, lambda i: (0,) * len(dims))

    return pl.pallas_call(
        functools.partial(spread_two_kernel, t),
        grid=(1,),
        in_specs=[SMEM] * 4
        + [full((F_W, V_F))] * F_DEV
        + [pl.BlockSpec((1, MAXT, TILE, TILE), lambda i: (t, 0, 0, 0))],
        out_specs=[full((F_W, V_F))] * F_DEV,
        out_shape=[CHUNK] * F_DEV,
        scratch_shapes=[
            pltpu.VMEM((BLOCKS + 1, F_W, TILE), f32),
            pltpu.VMEM((F_DEV, F_W, V_F), bf16),
        ],
        compiler_params=params(20),
        cost_estimate=cost(3),
        name="spread_two",
    )(me, counts, rows, cols, *h, tiles)


def relu_mix(me, parts, w_ref):
    weight = jnp.concatenate(
        [
            w_ref[pl.ds(pl.multiple_of(((me + F_DEV - k) % F_DEV) * F_W, F_W), F_W), :]
            for k in range(F_DEV)
        ],
        axis=0,
    )
    s = jnp.concatenate(parts, axis=0)
    return jnp.maximum(jnp.dot(weight.T, s, preferred_element_type=f32), 0.0)


def mix_one_kernel(me_ref, *refs):
    me = me_ref[0]
    in_refs, w_ref, whole_ref, out_refs = refs[:4], refs[4], refs[5], refs[6:]
    for k in range(F_DEV):
        start = pl.multiple_of(((me + F_DEV - k) % F_DEV) * F_W, F_W)
        whole_ref[pl.ds(start, F_W), :] = in_refs[k][0]
    mixed = relu_mix(me, [r[1] for r in in_refs], w_ref)
    whole_ref[...] = (whole_ref[...].astype(f32) + mixed).astype(bf16)
    for k in range(F_DEV):
        start = pl.multiple_of(((me + k) % F_DEV) * F_W, F_W)
        out_refs[k][...] = whole_ref[pl.ds(start, F_W), :]


def mix_one(me, parts, w):
    first, *rest = pl.pallas_call(
        mix_one_kernel,
        in_specs=[SMEM] + [VMEM] * 5,
        out_specs=[VMEM] * 5,
        out_shape=[jax.ShapeDtypeStruct((D, V_F), bf16)] + [CHUNK] * F_DEV,
        compiler_params=params(16),
        cost_estimate=cost(1),
        name="mix_one",
    )(me, *parts, w)
    return first, rest


def mix_two_kernel(last, me_ref, *refs):
    me = me_ref[0]
    s_refs, h_ref, w_ref, out_ref = refs[:4], refs[4], refs[5], refs[-1]
    mixed = relu_mix(me, [r[...] for r in s_refs], w_ref)
    h = (h_ref[...].astype(f32) + mixed).astype(bf16).T.reshape(S_DEV, V_S, D)
    if last:
        out_ref[:, :V_S, :] = refs[6][...]
        out_ref[:, V_S:, :] = h
    else:
        out_ref[...] = h


def mix_two(me, s, h, w, before):
    last = len(before)
    return pl.pallas_call(
        functools.partial(mix_two_kernel, last),
        in_specs=[SMEM] + [VMEM] * (6 + last),
        out_specs=VMEM,
        out_shape=jax.ShapeDtypeStruct((S_DEV, V_S * (1 + last), D), bf16),
        compiler_params=params(16),
        cost_estimate=cost(1),
        name="mix_two",
    )(me, *s, h, w, *before)


def attend_kernel(wq_ref, wk_ref, wv_ref, wo_ref, *refs):
    *h_refs, out_ref, hs, es, qt, vt, ks, ct = refs
    rows = SNAPS * V_S
    for parity in range(2):
        half = h_refs[parity][...] if len(h_refs) == 2 else h_refs[0][:, parity * V_S : (parity + 1) * V_S, :]
        for k in range(2):
            hs[k, parity] = half[:, :, k * 128 : (k + 1) * 128].reshape(S_DEV * V_S, 128).astype(f32)
    wqt = wq_ref[...].T
    wvt = wv_ref[...].T

    def project(c, _):
        at = pl.ds(pl.multiple_of(c * 4 * SNAPS, 4 * SNAPS), 4 * SNAPS)
        x = jnp.concatenate(
            [
                jnp.concatenate(
                    [hs[k, parity, pl.ds(c * 4 + v, S_DEV, stride=V_S), :] for k in range(2)], axis=1
                ).astype(bf16)
                for v in range(4)
                for parity in range(2)
            ],
            axis=0,
        )
        qt[:, at] = lax.dot_general(wqt, x, NT, preferred_element_type=f32).astype(bf16)
        vt[:, at] = lax.dot_general(wvt, x, NT, preferred_element_type=f32).astype(bf16)
        ks[at, :] = jnp.dot(x, wk_ref[...], preferred_element_type=f32).astype(bf16)
        return 0

    lax.fori_loop(0, rows // 512, project, 0, unroll=4)

    def time(dim):
        r = lax.broadcasted_iota(jnp.int32, (SNAPS, SNAPS), dim)
        return jnp.where(r < S_DEV, 2 * r, 2 * r - (SNAPS - 1))

    causal = time(0) <= time(1)
    scale = HEAD_DIM**-0.5 * LOG2_E

    def vertex(v, _):
        at = pl.ds(pl.multiple_of(v * SNAPS, SNAPS), SNAPS)
        key = ks[at, :]

        def padded(h):
            parts = [qt[h * HEAD_DIM : (h + 1) * HEAD_DIM, at]]
            if h > 0:
                parts.insert(0, jnp.zeros((h * HEAD_DIM, SNAPS), bf16))
            if h < HEADS - 1:
                parts.append(jnp.zeros((D - (h + 1) * HEAD_DIM, SNAPS), bf16))
            return jnp.concatenate(parts, axis=0)

        for pair in range(HEADS // 2):
            q_pair = jnp.concatenate([padded(2 * pair), padded(2 * pair + 1)], axis=1)
            scores = jnp.dot(key, q_pair, preferred_element_type=f32)
            for k in range(2):
                head = slice((2 * pair + k) * HEAD_DIM, (2 * pair + k + 1) * HEAD_DIM)
                s = jnp.where(causal, scores[:, k * SNAPS : (k + 1) * SNAPS], masked_score)
                top = jnp.max(s, axis=0, keepdims=True)
                lifted = jnp.exp2((s - top) * scale)
                total = jnp.sum(lifted, axis=0, keepdims=True)
                weights = (lifted * (1.0 / total)).astype(bf16)
                ct[head, at] = jnp.dot(
                    vt[head, at], weights, preferred_element_type=f32
                ).astype(bf16)
        return 0

    lax.fori_loop(0, V_S, vertex, 0, unroll=8)
    low = lax.broadcasted_iota(jnp.int32, (S_DEV, 128), 1) < F_W
    for v in range(V_S):
        at = pl.ds(v, S_DEV, stride=V_S)
        mixed = jnp.dot(
            ct[:, v * SNAPS : (v + 1) * SNAPS].T, wo_ref[...], preferred_element_type=f32
        )
        for k in range(2):
            even = hs[k, 0, at, :] + mixed[:S_DEV, k * 128 : (k + 1) * 128]
            odd = hs[k, 1, at, :] + mixed[S_DEV:, k * 128 : (k + 1) * 128]
            es[2 * k, at, :] = jnp.where(low, even, pltpu.roll(odd, F_W, 1))
            es[2 * k + 1, at, :] = jnp.where(low, pltpu.roll(even, F_W, 1), odd)
    for f in range(F_DEV):
        out_ref[f] = es[f].reshape(S_DEV, V_S, 128).astype(bf16)


def attend(wq, wk, wv, wo, *hidden):
    rows = SNAPS * V_S
    return pl.pallas_call(
        attend_kernel,
        out_shape=jax.ShapeDtypeStruct((F_DEV, S_DEV, V_S, 2 * F_W), bf16),
        scratch_shapes=[
            pltpu.VMEM((2, 2, S_DEV * V_S, 128), f32),
            pltpu.VMEM((F_DEV, S_DEV * V_S, 128), f32),
            pltpu.VMEM((D, rows), bf16),
            pltpu.VMEM((D, rows), bf16),
            pltpu.VMEM((rows, D), bf16),
            pltpu.VMEM((D, rows), bf16),
        ],
        compiler_params=params(32),
        name="attend",
    )(wq, wk, wv, wo, *hidden)


def place_kernel(in_ref, out_ref):
    for g in range(16):
        block = in_ref[g * 8 : (g + 1) * 8].reshape(128, 128).T
        out_ref[0, :, g * 128 : (g + 1) * 128] = block[:F_W]
        out_ref[1, :, g * 128 : (g + 1) * 128] = block[F_W:]


def place(pieces):
    return pl.pallas_call(
        place_kernel,
        grid=(2,),
        in_specs=[pl.BlockSpec((S_DEV * 2, V_S, 2 * F_W), lambda g: (g, 0, 0))],
        out_specs=pl.BlockSpec((2, F_W, V_F * 2), lambda g: (0, 0, g)),
        out_shape=jax.ShapeDtypeStruct((2, F_W, VERT), bf16),
        compiler_params=params(24),
        name="place",
    )(pieces)


def on_device(
    node_features,
    tile_rows,
    tile_cols,
    tile_counts,
    tile_values,
    layer_one,
    layer_two,
    query_weight,
    key_weight,
    value_weight,
    out_weight,
):
    x = jnp.swapaxes(node_features, 1, 2)
    me = lax.axis_index("feat").astype(jnp.int32).reshape(1)
    lists = (tile_values, tile_rows, tile_cols, tile_counts)

    both = range(2)
    s_one = [turn(spread_one(t, me, x, *lists)) for t in both]
    ones = [mix_one(me, s_one[t], layer_one) for t in both]
    h_one = [turn(ones[t][1]) for t in both]
    s_two = [turn(spread_two(t, me, h_one[t], *lists)) for t in both]
    hidden = []
    for t in both:
        hidden = [mix_two(me, s_two[t], ones[t][0], layer_two, hidden)]
    owned = lax.all_to_all(hidden[0], "snap", split_axis=0, concat_axis=0, tiled=True)
    evolved = attend(query_weight, key_weight, value_weight, out_weight, owned)
    pieces = lax.all_to_all(
        evolved.reshape(F_DEV * S_DEV, V_S, 2 * F_W),
        ("feat", "snap"),
        split_axis=0,
        concat_axis=0,
        tiled=True,
    )
    return jnp.swapaxes(place(pieces), 1, 2)


def solution(mesh):
    placed = (
        P("snap", None, "feat"),
        P("snap", None),
        P("snap", None),
        P("snap"),
        P("snap", None, None, None),
        P(),
        P(),
        P(),
        P(),
        P(),
        P(),
    )
    return jax.shard_map(
        on_device, mesh=mesh, in_specs=placed, out_specs=P("snap", None, "feat"), check_vma=False
    )
```

```python
import functools

import jax
import jax.numpy as jnp
from jax import lax
from jax.experimental import pallas as pl
from jax.experimental.pallas import tpu as pltpu
from jax.sharding import PartitionSpec as P

HEADS = 8
HEAD_DIM = 32
TILE = 128
D = 256
SNAPS = 128
VERT = 4096
BLOCKS = 32
MAXT = 64
F_DEV = 4
S_DEV = 64
F_W = D // F_DEV
V_F = VERT // F_DEV
V_S = V_F // S_DEV
GROUP = 8

masked_score = -1e30
LOG2_E = 1.4426950408889634
f32 = jnp.float32
bf16 = jnp.bfloat16
NT = (((1,), (1,)), ((), ()))
MIB = 2**20


def params(mib):
    return pltpu.CompilerParams(vmem_limit_bytes=mib * MIB)


GROUPS = MAXT // GROUP
SMEM = pl.BlockSpec(memory_space=pltpu.SMEM)
HBM = pl.BlockSpec(memory_space=pl.ANY)
VMEM = pl.BlockSpec(memory_space=pltpu.VMEM)
CHUNK = jax.ShapeDtypeStruct((F_W, V_F), bf16)
PAIR = jax.ShapeDtypeStruct((2, F_W, V_F), bf16)


def cost(us):
    return pl.CostEstimate(flops=int(us * 1e9), bytes_accessed=2**20, transcendentals=0)


def turn(blocks):
    sent = {
        k: lax.ppermute(blocks[k], "feat", [(i, (i + k) % F_DEV) for i in range(F_DEV)])
        for k in (2, 1, 3)
    }
    return [blocks[0], sent[1], sent[2], sent[3]]


def add_tiles(t, counts, rows, cols, features, tiles, acc, ready):
    n = counts[t]

    def group(g, _):
        ready(g)
        products = []
        for j in range(GROUP):
            i = g * GROUP + j
            products.append(
                lax.dot_general(features(cols[t, i]), tiles(i), NT, preferred_element_type=f32)
            )
        for j in range(GROUP):
            i = g * GROUP + j
            row = jnp.where(i < n, rows[t, i], BLOCKS)
            acc[row] += products[j]
        return 0

    lax.fori_loop(0, (n + GROUP - 1) // GROUP, group, 0)


def spread_one_kernel(t, me_ref, counts, rows, cols, x_hbm, tiles_hbm, *refs):
    out_refs, (acc, x, tiles, x_sem, sems) = refs[:F_DEV], refs[F_DEV:]
    me = me_ref[0]
    fetch_x = pltpu.make_async_copy(x_hbm.at[t], x, x_sem)
    fetch_x.start()

    def fetch(g):
        at = pl.ds(g * GROUP, GROUP)
        return pltpu.make_async_copy(tiles_hbm.at[t, at], tiles.at[at], sems.at[g])

    def start(g, _):
        fetch(g).start()
        return 0

    lax.fori_loop(0, (counts[t] + GROUP - 1) // GROUP, start, 0)
    acc[...] = jnp.zeros_like(acc)
    fetch_x.wait()
    for k in range(F_DEV):
        block = (me + k) % F_DEV
        out_refs[k][0] = x[:, pl.ds(pl.multiple_of(block * V_F, V_F), V_F)]
    add_tiles(
        t,
        counts,
        rows,
        cols,
        lambda col: x[:, pl.ds(pl.multiple_of(col * TILE, TILE), TILE)],
        lambda i: tiles[i],
        acc,
        lambda g: fetch(g).wait(),
    )
    for k in range(F_DEV):
        block = (me + k) % F_DEV
        for b in range(8):
            out_refs[k][1, :, b * TILE : (b + 1) * TILE] = acc[block * 8 + b].astype(bf16)


def spread_one(t, me, x, tiles, rows, cols, counts):
    return pl.pallas_call(
        functools.partial(spread_one_kernel, t),
        in_specs=[SMEM] * 4 + [HBM] * 2,
        out_specs=[VMEM] * F_DEV,
        out_shape=[PAIR] * F_DEV,
        scratch_shapes=[
            pltpu.VMEM((BLOCKS + 1, F_W, TILE), f32),
            pltpu.VMEM((F_W, VERT), bf16),
            pltpu.VMEM((MAXT, TILE, TILE), bf16),
            pltpu.SemaphoreType.DMA,
            pltpu.SemaphoreType.DMA((GROUPS,)),
        ],
        compiler_params=params(SPREAD_MIB[t]),
        cost_estimate=cost(4),
        name="spread_one",
    )(me, counts, rows, cols, x, tiles)


SPREAD_MIB = (56, 52)


def spread_two_kernel(t, me_ref, counts, rows, cols, *refs):
    h_refs, tiles, out_refs, (acc, h) = refs[:4], refs[4], refs[5:9], refs[9:]
    me = me_ref[0]
    for k in range(F_DEV):
        h[(me + F_DEV - k) % F_DEV] = h_refs[k][...]
    acc[...] = jnp.zeros_like(acc)
    add_tiles(
        t,
        counts,
        rows,
        cols,
        lambda col: h[col // 8, :, pl.ds(pl.multiple_of((col % 8) * TILE, TILE), TILE)],
        lambda i: tiles[0, i],
        acc,
        lambda g: None,
    )
    for k in range(F_DEV):
        block = (me + k) % F_DEV
        for b in range(8):
            out_refs[k][:, b * TILE : (b + 1) * TILE] = acc[block * 8 + b].astype(bf16)


def spread_two(t, me, h, tiles, rows, cols, counts):
    def full(dims):
        return pl.BlockSpec(dims, lambda i: (0,) * len(dims))

    return pl.pallas_call(
        functools.partial(spread_two_kernel, t),
        grid=(1,),
        in_specs=[SMEM] * 4
        + [full((F_W, V_F))] * F_DEV
        + [pl.BlockSpec((1, MAXT, TILE, TILE), lambda i: (t, 0, 0, 0))],
        out_specs=[full((F_W, V_F))] * F_DEV,
        out_shape=[CHUNK] * F_DEV,
        scratch_shapes=[
            pltpu.VMEM((BLOCKS + 1, F_W, TILE), f32),
            pltpu.VMEM((F_DEV, F_W, V_F), bf16),
        ],
        compiler_params=params(20),
        cost_estimate=cost(3),
        name="spread_two",
    )(me, counts, rows, cols, *h, tiles)


def relu_mix(me, parts, w_ref):
    weight = jnp.concatenate(
        [
            w_ref[pl.ds(pl.multiple_of(((me + F_DEV - k) % F_DEV) * F_W, F_W), F_W), :]
            for k in range(F_DEV)
        ],
        axis=0,
    )
    s = jnp.concatenate(parts, axis=0)
    return jnp.maximum(jnp.dot(weight.T, s, preferred_element_type=f32), 0.0)


def mix_one_kernel(me_ref, *refs):
    me = me_ref[0]
    in_refs, w_ref, whole_ref, out_refs = refs[:4], refs[4], refs[5], refs[6:]
    for k in range(F_DEV):
        start = pl.multiple_of(((me + F_DEV - k) % F_DEV) * F_W, F_W)
        whole_ref[pl.ds(start, F_W), :] = in_refs[k][0]
    mixed = relu_mix(me, [r[1] for r in in_refs], w_ref)
    whole_ref[...] = (whole_ref[...].astype(f32) + mixed).astype(bf16)
    for k in range(F_DEV):
        start = pl.multiple_of(((me + k) % F_DEV) * F_W, F_W)
        out_refs[k][...] = whole_ref[pl.ds(start, F_W), :]


def mix_one(me, parts, w):
    first, *rest = pl.pallas_call(
        mix_one_kernel,
        in_specs=[SMEM] + [VMEM] * 5,
        out_specs=[VMEM] * 5,
        out_shape=[jax.ShapeDtypeStruct((D, V_F), bf16)] + [CHUNK] * F_DEV,
        compiler_params=params(16),
        cost_estimate=cost(1),
        name="mix_one",
    )(me, *parts, w)
    return first, rest


def mix_two_kernel(last, me_ref, *refs):
    me = me_ref[0]
    s_refs, h_ref, w_ref, out_ref = refs[:4], refs[4], refs[5], refs[-1]
    mixed = relu_mix(me, [r[...] for r in s_refs], w_ref)
    h = (h_ref[...].astype(f32) + mixed).astype(bf16).T.reshape(S_DEV, V_S, D)
    if last:
        out_ref[:, :V_S, :] = refs[6][...]
        out_ref[:, V_S:, :] = h
    else:
        out_ref[...] = h


def mix_two(me, s, h, w, before):
    last = len(before)
    return pl.pallas_call(
        functools.partial(mix_two_kernel, last),
        in_specs=[SMEM] + [VMEM] * (6 + last),
        out_specs=VMEM,
        out_shape=jax.ShapeDtypeStruct((S_DEV, V_S * (1 + last), D), bf16),
        compiler_params=params(16),
        cost_estimate=cost(1),
        name="mix_two",
    )(me, *s, h, w, *before)


def attend_kernel(wq_ref, wk_ref, wv_ref, wo_ref, *refs):
    *h_refs, out_ref, hs, es, qt, vt, ks, ct = refs
    rows = SNAPS * V_S
    for parity in range(2):
        half = h_refs[parity][...] if len(h_refs) == 2 else h_refs[0][:, parity * V_S : (parity + 1) * V_S, :]
        for k in range(2):
            hs[k, parity] = half[:, :, k * 128 : (k + 1) * 128].reshape(S_DEV * V_S, 128).astype(f32)
    wqt = wq_ref[...].T
    wvt = wv_ref[...].T

    def project(c, _):
        at = pl.ds(pl.multiple_of(c * 4 * SNAPS, 4 * SNAPS), 4 * SNAPS)
        x = jnp.concatenate(
            [
                jnp.concatenate(
                    [hs[k, parity, pl.ds(c * 4 + v, S_DEV, stride=V_S), :] for k in range(2)], axis=1
                ).astype(bf16)
                for v in range(4)
                for parity in range(2)
            ],
            axis=0,
        )
        qt[:, at] = lax.dot_general(wqt, x, NT, preferred_element_type=f32).astype(bf16)
        vt[:, at] = lax.dot_general(wvt, x, NT, preferred_element_type=f32).astype(bf16)
        ks[at, :] = jnp.dot(x, wk_ref[...], preferred_element_type=f32).astype(bf16)
        return 0

    lax.fori_loop(0, rows // 512, project, 0, unroll=4)

    def time(dim):
        r = lax.broadcasted_iota(jnp.int32, (SNAPS, SNAPS), dim)
        return jnp.where(r < S_DEV, 2 * r, 2 * r - (SNAPS - 1))

    causal = time(0) <= time(1)
    scale = HEAD_DIM**-0.5 * LOG2_E

    def vertex(v, _):
        at = pl.ds(pl.multiple_of(v * SNAPS, SNAPS), SNAPS)
        key = ks[at, :]

        def padded(h):
            parts = [qt[h * HEAD_DIM : (h + 1) * HEAD_DIM, at]]
            if h > 0:
                parts.insert(0, jnp.zeros((h * HEAD_DIM, SNAPS), bf16))
            if h < HEADS - 1:
                parts.append(jnp.zeros((D - (h + 1) * HEAD_DIM, SNAPS), bf16))
            return jnp.concatenate(parts, axis=0)

        for pair in range(HEADS // 2):
            q_pair = jnp.concatenate([padded(2 * pair), padded(2 * pair + 1)], axis=1)
            scores = jnp.dot(key, q_pair, preferred_element_type=f32)
            for k in range(2):
                head = slice((2 * pair + k) * HEAD_DIM, (2 * pair + k + 1) * HEAD_DIM)
                s = jnp.where(causal, scores[:, k * SNAPS : (k + 1) * SNAPS], masked_score)
                top = jnp.max(s, axis=0, keepdims=True)
                lifted = jnp.exp2((s - top) * scale)
                total = jnp.sum(lifted, axis=0, keepdims=True)
                weights = (lifted * (1.0 / total)).astype(bf16)
                ct[head, at] = jnp.dot(
                    vt[head, at], weights, preferred_element_type=f32
                ).astype(bf16)
        return 0

    lax.fori_loop(0, V_S, vertex, 0, unroll=8)
    low = lax.broadcasted_iota(jnp.int32, (S_DEV, 128), 1) < F_W
    for v in range(V_S):
        at = pl.ds(v, S_DEV, stride=V_S)
        mixed = jnp.dot(
            ct[:, v * SNAPS : (v + 1) * SNAPS].T, wo_ref[...], preferred_element_type=f32
        )
        for k in range(2):
            even = hs[k, 0, at, :] + mixed[:S_DEV, k * 128 : (k + 1) * 128]
            odd = hs[k, 1, at, :] + mixed[S_DEV:, k * 128 : (k + 1) * 128]
            es[2 * k, at, :] = jnp.where(low, even, pltpu.roll(odd, F_W, 1))
            es[2 * k + 1, at, :] = jnp.where(low, pltpu.roll(even, F_W, 1), odd)
    for f in range(F_DEV):
        out_ref[f] = es[f].reshape(S_DEV, V_S, 128).astype(bf16)


def attend(wq, wk, wv, wo, *hidden):
    rows = SNAPS * V_S
    return pl.pallas_call(
        attend_kernel,
        out_shape=jax.ShapeDtypeStruct((F_DEV, S_DEV, V_S, 2 * F_W), bf16),
        scratch_shapes=[
            pltpu.VMEM((2, 2, S_DEV * V_S, 128), f32),
            pltpu.VMEM((F_DEV, S_DEV * V_S, 128), f32),
            pltpu.VMEM((D, rows), bf16),
            pltpu.VMEM((D, rows), bf16),
            pltpu.VMEM((rows, D), bf16),
            pltpu.VMEM((D, rows), bf16),
        ],
        compiler_params=params(32),
        name="attend",
    )(wq, wk, wv, wo, *hidden)


def place_kernel(in_ref, out_ref):
    for g in range(16):
        block = in_ref[g * 8 : (g + 1) * 8].reshape(128, 128).T
        out_ref[0, :, g * 128 : (g + 1) * 128] = block[:F_W]
        out_ref[1, :, g * 128 : (g + 1) * 128] = block[F_W:]


def place(pieces):
    return pl.pallas_call(
        place_kernel,
        grid=(2,),
        in_specs=[pl.BlockSpec((S_DEV * 2, V_S, 2 * F_W), lambda g: (g, 0, 0))],
        out_specs=pl.BlockSpec((2, F_W, V_F * 2), lambda g: (0, 0, g)),
        out_shape=jax.ShapeDtypeStruct((2, F_W, VERT), bf16),
        compiler_params=params(24),
        name="place",
    )(pieces)


def on_device(
    node_features,
    tile_rows,
    tile_cols,
    tile_counts,
    tile_values,
    layer_one,
    layer_two,
    query_weight,
    key_weight,
    value_weight,
    out_weight,
):
    x = jnp.swapaxes(node_features, 1, 2)
    me = lax.axis_index("feat").astype(jnp.int32).reshape(1)
    lists = (tile_values, tile_rows, tile_cols, tile_counts)

    both = range(2)
    s_one = [turn(spread_one(t, me, x, *lists)) for t in both]
    ones = [mix_one(me, s_one[t], layer_one) for t in both]
    h_one = [turn(ones[t][1]) for t in both]
    s_two = [turn(spread_two(t, me, h_one[t], *lists)) for t in both]
    hidden = []
    for t in both:
        hidden = [mix_two(me, s_two[t], ones[t][0], layer_two, hidden)]
    owned = lax.all_to_all(hidden[0], "snap", split_axis=0, concat_axis=0, tiled=True)
    evolved = attend(query_weight, key_weight, value_weight, out_weight, owned)
    pieces = lax.all_to_all(
        evolved.reshape(F_DEV * S_DEV, V_S, 2 * F_W),
        ("feat", "snap"),
        split_axis=0,
        concat_axis=0,
        tiled=True,
    )
    return jnp.swapaxes(place(pieces), 1, 2)


def solution(mesh):
    placed = (
        P("snap", None, "feat"),
        P("snap", None),
        P("snap", None),
        P("snap"),
        P("snap", None, None, None),
        P(),
        P(),
        P(),
        P(),
        P(),
        P(),
    )
    return jax.shard_map(
        on_device, mesh=mesh, in_specs=placed, out_specs=P("snap", None, "feat"), check_vma=False
    )
```

```python
import functools

import jax
import jax.numpy as jnp
from jax import lax
from jax.experimental import pallas as pl
from jax.experimental.pallas import tpu as pltpu
from jax.sharding import PartitionSpec as P

HEADS = 8
HEAD_DIM = 32
TILE = 128
D = 256
SNAPS = 128
VERT = 4096
BLOCKS = 32
MAXT = 64
F_DEV = 4
S_DEV = 64
F_W = D // F_DEV
V_F = VERT // F_DEV
V_S = V_F // S_DEV
GROUP = 8

masked_score = -1e30
LOG2_E = 1.4426950408889634
f32 = jnp.float32
bf16 = jnp.bfloat16
NT = (((1,), (1,)), ((), ()))
MIB = 2**20


def params(mib):
    return pltpu.CompilerParams(vmem_limit_bytes=mib * MIB)


GROUPS = MAXT // GROUP
SMEM = pl.BlockSpec(memory_space=pltpu.SMEM)
HBM = pl.BlockSpec(memory_space=pl.ANY)
VMEM = pl.BlockSpec(memory_space=pltpu.VMEM)
CHUNK = jax.ShapeDtypeStruct((F_W, V_F), bf16)
PAIR = jax.ShapeDtypeStruct((2, F_W, V_F), bf16)


def cost(us):
    return pl.CostEstimate(flops=int(us * 1e9), bytes_accessed=2**20, transcendentals=0)


def turn(blocks):
    sent = {
        k: lax.ppermute(blocks[k], "feat", [(i, (i + k) % F_DEV) for i in range(F_DEV)])
        for k in (2, 1, 3)
    }
    return [blocks[0], sent[1], sent[2], sent[3]]


def add_tiles(t, counts, rows, cols, features, tiles, acc, ready):
    n = counts[t]
    acc[...] = jnp.zeros_like(acc)

    def group(g, _):
        ready(g)
        products = []
        for j in range(GROUP):
            i = g * GROUP + j
            products.append(
                lax.dot_general(features(cols[t, i]), tiles(i), NT, preferred_element_type=f32)
            )
        for j in range(GROUP):
            i = g * GROUP + j
            row = jnp.where(i < n, rows[t, i], BLOCKS)
            acc[row] += products[j]
        return 0

    lax.fori_loop(0, (n + GROUP - 1) // GROUP, group, 0)


def spread_one_kernel(t, me_ref, counts, rows, cols, x_hbm, tiles_hbm, *refs):
    out_refs, (acc, x, tiles, x_sem, sems) = refs[:F_DEV], refs[F_DEV:]
    me = me_ref[0]
    fetch_x = pltpu.make_async_copy(x_hbm.at[t], x, x_sem)
    fetch_x.start()

    def fetch(g):
        at = pl.ds(g * GROUP, GROUP)
        return pltpu.make_async_copy(tiles_hbm.at[t, at], tiles.at[at], sems.at[g])

    def start(g, _):
        fetch(g).start()
        return 0

    lax.fori_loop(0, (counts[t] + GROUP - 1) // GROUP, start, 0)
    fetch_x.wait()
    add_tiles(
        t,
        counts,
        rows,
        cols,
        lambda col: x[:, pl.ds(pl.multiple_of(col * TILE, TILE), TILE)],
        lambda i: tiles[i],
        acc,
        lambda g: fetch(g).wait(),
    )
    for k in range(F_DEV):
        block = (me + k) % F_DEV
        out_refs[k][0] = x[:, pl.ds(pl.multiple_of(block * V_F, V_F), V_F)]
        for b in range(8):
            out_refs[k][1, :, b * TILE : (b + 1) * TILE] = acc[block * 8 + b].astype(bf16)


def spread_one(t, me, x, tiles, rows, cols, counts):
    return pl.pallas_call(
        functools.partial(spread_one_kernel, t),
        in_specs=[SMEM] * 4 + [HBM] * 2,
        out_specs=[VMEM] * F_DEV,
        out_shape=[PAIR] * F_DEV,
        scratch_shapes=[
            pltpu.VMEM((BLOCKS + 1, F_W, TILE), f32),
            pltpu.VMEM((F_W, VERT), bf16),
            pltpu.VMEM((MAXT, TILE, TILE), bf16),
            pltpu.SemaphoreType.DMA,
            pltpu.SemaphoreType.DMA((GROUPS,)),
        ],
        compiler_params=params(SPREAD_MIB[t]),
        cost_estimate=cost(4),
        name="spread_one",
    )(me, counts, rows, cols, x, tiles)


SPREAD_MIB = (56, 52)


def spread_two_kernel(t, me_ref, counts, rows, cols, *refs):
    h_refs, tiles, out_refs, (acc, h) = refs[:4], refs[4], refs[5:9], refs[9:]
    me = me_ref[0]
    for k in range(F_DEV):
        h[(me + F_DEV - k) % F_DEV] = h_refs[k][...]
    add_tiles(
        t,
        counts,
        rows,
        cols,
        lambda col: h[col // 8, :, pl.ds(pl.multiple_of((col % 8) * TILE, TILE), TILE)],
        lambda i: tiles[0, i],
        acc,
        lambda g: None,
    )
    for k in range(F_DEV):
        block = (me + k) % F_DEV
        for b in range(8):
            out_refs[k][:, b * TILE : (b + 1) * TILE] = acc[block * 8 + b].astype(bf16)


def spread_two(t, me, h, tiles, rows, cols, counts):
    def full(dims):
        return pl.BlockSpec(dims, lambda i: (0,) * len(dims))

    return pl.pallas_call(
        functools.partial(spread_two_kernel, t),
        grid=(1,),
        in_specs=[SMEM] * 4
        + [full((F_W, V_F))] * F_DEV
        + [pl.BlockSpec((1, MAXT, TILE, TILE), lambda i: (t, 0, 0, 0))],
        out_specs=[full((F_W, V_F))] * F_DEV,
        out_shape=[CHUNK] * F_DEV,
        scratch_shapes=[
            pltpu.VMEM((BLOCKS + 1, F_W, TILE), f32),
            pltpu.VMEM((F_DEV, F_W, V_F), bf16),
        ],
        compiler_params=params(20),
        cost_estimate=cost(3),
        name="spread_two",
    )(me, counts, rows, cols, *h, tiles)


def relu_mix(me, parts, w_ref):
    weight = jnp.concatenate(
        [
            w_ref[pl.ds(pl.multiple_of(((me + F_DEV - k) % F_DEV) * F_W, F_W), F_W), :]
            for k in range(F_DEV)
        ],
        axis=0,
    )
    s = jnp.concatenate(parts, axis=0)
    return jnp.maximum(jnp.dot(weight.T, s, preferred_element_type=f32), 0.0)


def mix_one_kernel(me_ref, *refs):
    me = me_ref[0]
    in_refs, w_ref, whole_ref, out_refs = refs[:4], refs[4], refs[5], refs[6:]
    for k in range(F_DEV):
        start = pl.multiple_of(((me + F_DEV - k) % F_DEV) * F_W, F_W)
        whole_ref[pl.ds(start, F_W), :] = in_refs[k][0]
    mixed = relu_mix(me, [r[1] for r in in_refs], w_ref)
    whole_ref[...] = (whole_ref[...].astype(f32) + mixed).astype(bf16)
    for k in range(F_DEV):
        start = pl.multiple_of(((me + k) % F_DEV) * F_W, F_W)
        out_refs[k][...] = whole_ref[pl.ds(start, F_W), :]


def mix_one(me, parts, w):
    first, *rest = pl.pallas_call(
        mix_one_kernel,
        in_specs=[SMEM] + [VMEM] * 5,
        out_specs=[VMEM] * 5,
        out_shape=[jax.ShapeDtypeStruct((D, V_F), bf16)] + [CHUNK] * F_DEV,
        compiler_params=params(16),
        cost_estimate=cost(1),
        name="mix_one",
    )(me, *parts, w)
    return first, rest


def mix_two_kernel(last, me_ref, *refs):
    me = me_ref[0]
    s_refs, h_ref, w_ref, out_ref = refs[:4], refs[4], refs[5], refs[-1]
    mixed = relu_mix(me, [r[...] for r in s_refs], w_ref)
    h = (h_ref[...].astype(f32) + mixed).astype(bf16).T.reshape(S_DEV, V_S, D)
    if last:
        out_ref[:, :V_S, :] = refs[6][...]
        out_ref[:, V_S:, :] = h
    else:
        out_ref[...] = h


def mix_two(me, s, h, w, before):
    last = len(before)
    return pl.pallas_call(
        functools.partial(mix_two_kernel, last),
        in_specs=[SMEM] + [VMEM] * (6 + last),
        out_specs=VMEM,
        out_shape=jax.ShapeDtypeStruct((S_DEV, V_S * (1 + last), D), bf16),
        compiler_params=params(16),
        cost_estimate=cost(1),
        name="mix_two",
    )(me, *s, h, w, *before)


def attend_kernel(wq_ref, wk_ref, wv_ref, wo_ref, *refs):
    *h_refs, out_ref, hs, es, qt, vt, ks, ct = refs
    rows = SNAPS * V_S
    for parity in range(2):
        half = h_refs[parity][...] if len(h_refs) == 2 else h_refs[0][:, parity * V_S : (parity + 1) * V_S, :]
        for k in range(2):
            hs[k, parity] = half[:, :, k * 128 : (k + 1) * 128].reshape(S_DEV * V_S, 128).astype(f32)
    wqt = wq_ref[...].T
    wvt = wv_ref[...].T

    def project(c, _):
        at = pl.ds(pl.multiple_of(c * 4 * SNAPS, 4 * SNAPS), 4 * SNAPS)
        x = jnp.concatenate(
            [
                jnp.concatenate(
                    [hs[k, parity, pl.ds(c * 4 + v, S_DEV, stride=V_S), :] for k in range(2)], axis=1
                ).astype(bf16)
                for v in range(4)
                for parity in range(2)
            ],
            axis=0,
        )
        qt[:, at] = lax.dot_general(wqt, x, NT, preferred_element_type=f32).astype(bf16)
        vt[:, at] = lax.dot_general(wvt, x, NT, preferred_element_type=f32).astype(bf16)
        ks[at, :] = jnp.dot(x, wk_ref[...], preferred_element_type=f32).astype(bf16)
        return 0

    lax.fori_loop(0, rows // 512, project, 0, unroll=4)

    def time(dim):
        r = lax.broadcasted_iota(jnp.int32, (SNAPS, SNAPS), dim)
        return jnp.where(r < S_DEV, 2 * r, 2 * r - (SNAPS - 1))

    causal = time(0) <= time(1)
    scale = HEAD_DIM**-0.5 * LOG2_E

    def vertex(v, _):
        at = pl.ds(pl.multiple_of(v * SNAPS, SNAPS), SNAPS)
        key = ks[at, :]

        def padded(h):
            parts = [qt[h * HEAD_DIM : (h + 1) * HEAD_DIM, at]]
            if h > 0:
                parts.insert(0, jnp.zeros((h * HEAD_DIM, SNAPS), bf16))
            if h < HEADS - 1:
                parts.append(jnp.zeros((D - (h + 1) * HEAD_DIM, SNAPS), bf16))
            return jnp.concatenate(parts, axis=0)

        for pair in range(HEADS // 2):
            q_pair = jnp.concatenate([padded(2 * pair), padded(2 * pair + 1)], axis=1)
            scores = jnp.dot(key, q_pair, preferred_element_type=f32)
            for k in range(2):
                head = slice((2 * pair + k) * HEAD_DIM, (2 * pair + k + 1) * HEAD_DIM)
                s = jnp.where(causal, scores[:, k * SNAPS : (k + 1) * SNAPS], masked_score)
                top = jnp.max(s, axis=0, keepdims=True)
                lifted = jnp.exp2((s - top) * scale)
                total = jnp.sum(lifted, axis=0, keepdims=True)
                weights = (lifted * (1.0 / total)).astype(bf16)
                ct[head, at] = jnp.dot(
                    vt[head, at], weights, preferred_element_type=f32
                ).astype(bf16)
        return 0

    lax.fori_loop(0, V_S, vertex, 0, unroll=8)
    low = lax.broadcasted_iota(jnp.int32, (S_DEV, 128), 1) < F_W
    for v in range(V_S):
        at = pl.ds(v, S_DEV, stride=V_S)
        mixed = jnp.dot(
            ct[:, v * SNAPS : (v + 1) * SNAPS].T, wo_ref[...], preferred_element_type=f32
        )
        for k in range(2):
            even = hs[k, 0, at, :] + mixed[:S_DEV, k * 128 : (k + 1) * 128]
            odd = hs[k, 1, at, :] + mixed[S_DEV:, k * 128 : (k + 1) * 128]
            es[2 * k, at, :] = jnp.where(low, even, pltpu.roll(odd, F_W, 1))
            es[2 * k + 1, at, :] = jnp.where(low, pltpu.roll(even, F_W, 1), odd)
    for f in range(F_DEV):
        out_ref[f] = es[f].reshape(S_DEV, V_S, 128).astype(bf16)


def attend(wq, wk, wv, wo, *hidden):
    rows = SNAPS * V_S
    return pl.pallas_call(
        attend_kernel,
        out_shape=jax.ShapeDtypeStruct((F_DEV, S_DEV, V_S, 2 * F_W), bf16),
        scratch_shapes=[
            pltpu.VMEM((2, 2, S_DEV * V_S, 128), f32),
            pltpu.VMEM((F_DEV, S_DEV * V_S, 128), f32),
            pltpu.VMEM((D, rows), bf16),
            pltpu.VMEM((D, rows), bf16),
            pltpu.VMEM((rows, D), bf16),
            pltpu.VMEM((D, rows), bf16),
        ],
        compiler_params=params(32),
        name="attend",
    )(wq, wk, wv, wo, *hidden)


def place_kernel(in_ref, out_ref):
    for g in range(16):
        block = in_ref[g * 8 : (g + 1) * 8].reshape(128, 128).T
        out_ref[0, :, g * 128 : (g + 1) * 128] = block[:F_W]
        out_ref[1, :, g * 128 : (g + 1) * 128] = block[F_W:]


def place(pieces):
    return pl.pallas_call(
        place_kernel,
        grid=(2,),
        in_specs=[pl.BlockSpec((S_DEV * 2, V_S, 2 * F_W), lambda g: (g, 0, 0))],
        out_specs=pl.BlockSpec((2, F_W, V_F * 2), lambda g: (0, 0, g)),
        out_shape=jax.ShapeDtypeStruct((2, F_W, VERT), bf16),
        compiler_params=params(24),
        name="place",
    )(pieces)


def on_device(
    node_features,
    tile_rows,
    tile_cols,
    tile_counts,
    tile_values,
    layer_one,
    layer_two,
    query_weight,
    key_weight,
    value_weight,
    out_weight,
):
    x = jnp.swapaxes(node_features, 1, 2)
    me = lax.axis_index("feat").astype(jnp.int32).reshape(1)
    lists = (tile_values, tile_rows, tile_cols, tile_counts)

    both = range(2)
    s_one = [turn(spread_one(0, me, x, *lists))]
    other = list(spread_one(1, me, x, *lists))
    ones = [mix_one(me, s_one[0], layer_one)]
    other[2], _ = lax.optimization_barrier((other[2], ones[0][1][0]))
    s_one.append(turn(other))
    ones.append(mix_one(me, s_one[1], layer_one))
    h_one = [turn(ones[t][1]) for t in both]
    s_two = [turn(spread_two(t, me, h_one[t], *lists)) for t in both]
    hidden = []
    for t in both:
        hidden = [mix_two(me, s_two[t], ones[t][0], layer_two, hidden)]
    owned = lax.all_to_all(hidden[0], "snap", split_axis=0, concat_axis=0, tiled=True)
    evolved = attend(query_weight, key_weight, value_weight, out_weight, owned)
    pieces = lax.all_to_all(
        evolved.reshape(F_DEV * S_DEV, V_S, 2 * F_W),
        ("feat", "snap"),
        split_axis=0,
        concat_axis=0,
        tiled=True,
    )
    return jnp.swapaxes(place(pieces), 1, 2)


def solution(mesh):
    placed = (
        P("snap", None, "feat"),
        P("snap", None),
        P("snap", None),
        P("snap"),
        P("snap", None, None, None),
        P(),
        P(),
        P(),
        P(),
        P(),
        P(),
    )
    return jax.shard_map(
        on_device, mesh=mesh, in_specs=placed, out_specs=P("snap", None, "feat"), check_vma=False
    )
```

```python
import functools

import jax
import jax.numpy as jnp
from jax import lax
from jax.experimental import pallas as pl
from jax.experimental.pallas import tpu as pltpu
from jax.sharding import PartitionSpec as P

HEADS = 8
HEAD_DIM = 32
TILE = 128
D = 256
SNAPS = 128
VERT = 4096
BLOCKS = 32
MAXT = 64
F_DEV = 4
S_DEV = 64
F_W = D // F_DEV
V_F = VERT // F_DEV
V_S = V_F // S_DEV
GROUP = 16

masked_score = -1e30
LOG2_E = 1.4426950408889634
f32 = jnp.float32
bf16 = jnp.bfloat16
NT = (((1,), (1,)), ((), ()))
MIB = 2**20


def params(mib):
    return pltpu.CompilerParams(vmem_limit_bytes=mib * MIB)


GROUPS = MAXT // GROUP
SMEM = pl.BlockSpec(memory_space=pltpu.SMEM)
HBM = pl.BlockSpec(memory_space=pl.ANY)
VMEM = pl.BlockSpec(memory_space=pltpu.VMEM)
CHUNK = jax.ShapeDtypeStruct((F_W, V_F), bf16)
PAIR = jax.ShapeDtypeStruct((2, F_W, V_F), bf16)


def cost(us):
    return pl.CostEstimate(flops=int(us * 1e9), bytes_accessed=2**20, transcendentals=0)


def turn(blocks):
    sent = {
        k: lax.ppermute(blocks[k], "feat", [(i, (i + k) % F_DEV) for i in range(F_DEV)])
        for k in (2, 1, 3)
    }
    return [blocks[0], sent[1], sent[2], sent[3]]


def add_tiles(t, counts, rows, cols, features, tiles, acc, ready):
    n = counts[t]
    acc[...] = jnp.zeros_like(acc)

    def group(g, _):
        ready(g)
        products = []
        for j in range(GROUP):
            i = g * GROUP + j
            products.append(
                lax.dot_general(features(cols[t, i]), tiles(i), NT, preferred_element_type=f32)
            )
        for j in range(GROUP):
            i = g * GROUP + j
            row = jnp.where(i < n, rows[t, i], BLOCKS)
            acc[row] += products[j]
        return 0

    lax.fori_loop(0, (n + GROUP - 1) // GROUP, group, 0)


def spread_one_kernel(t, me_ref, counts, rows, cols, x_hbm, tiles_hbm, *refs):
    out_refs, (acc, x, tiles, x_sem, sems) = refs[:F_DEV], refs[F_DEV:]
    me = me_ref[0]
    fetch_x = pltpu.make_async_copy(x_hbm.at[t], x, x_sem)
    fetch_x.start()

    def fetch(g):
        at = pl.ds(g * GROUP, GROUP)
        return pltpu.make_async_copy(tiles_hbm.at[t, at], tiles.at[at], sems.at[g])

    def start(g, _):
        fetch(g).start()
        return 0

    lax.fori_loop(0, (counts[t] + GROUP - 1) // GROUP, start, 0)
    fetch_x.wait()
    add_tiles(
        t,
        counts,
        rows,
        cols,
        lambda col: x[:, pl.ds(pl.multiple_of(col * TILE, TILE), TILE)],
        lambda i: tiles[i],
        acc,
        lambda g: fetch(g).wait(),
    )
    for k in range(F_DEV):
        block = (me + k) % F_DEV
        out_refs[k][0] = x[:, pl.ds(pl.multiple_of(block * V_F, V_F), V_F)]
        for b in range(8):
            out_refs[k][1, :, b * TILE : (b + 1) * TILE] = acc[block * 8 + b].astype(bf16)


def spread_one(t, me, x, tiles, rows, cols, counts):
    return pl.pallas_call(
        functools.partial(spread_one_kernel, t),
        in_specs=[SMEM] * 4 + [HBM] * 2,
        out_specs=[VMEM] * F_DEV,
        out_shape=[PAIR] * F_DEV,
        scratch_shapes=[
            pltpu.VMEM((BLOCKS + 1, F_W, TILE), f32),
            pltpu.VMEM((F_W, VERT), bf16),
            pltpu.VMEM((MAXT, TILE, TILE), bf16),
            pltpu.SemaphoreType.DMA,
            pltpu.SemaphoreType.DMA((GROUPS,)),
        ],
        compiler_params=params(SPREAD_MIB[t]),
        cost_estimate=cost(4),
        name="spread_one",
    )(me, counts, rows, cols, x, tiles)


SPREAD_MIB = (56, 52)


def spread_two_kernel(t, me_ref, counts, rows, cols, *refs):
    h_refs, tiles, out_refs, (acc, h) = refs[:4], refs[4], refs[5:9], refs[9:]
    me = me_ref[0]
    for k in range(F_DEV):
        h[(me + F_DEV - k) % F_DEV] = h_refs[k][...]
    add_tiles(
        t,
        counts,
        rows,
        cols,
        lambda col: h[col // 8, :, pl.ds(pl.multiple_of((col % 8) * TILE, TILE), TILE)],
        lambda i: tiles[0, i],
        acc,
        lambda g: None,
    )
    for k in range(F_DEV):
        block = (me + k) % F_DEV
        for b in range(8):
            out_refs[k][:, b * TILE : (b + 1) * TILE] = acc[block * 8 + b].astype(bf16)


def spread_two(t, me, h, tiles, rows, cols, counts):
    def full(dims):
        return pl.BlockSpec(dims, lambda i: (0,) * len(dims))

    return pl.pallas_call(
        functools.partial(spread_two_kernel, t),
        grid=(1,),
        in_specs=[SMEM] * 4
        + [full((F_W, V_F))] * F_DEV
        + [pl.BlockSpec((1, MAXT, TILE, TILE), lambda i: (t, 0, 0, 0))],
        out_specs=[full((F_W, V_F))] * F_DEV,
        out_shape=[CHUNK] * F_DEV,
        scratch_shapes=[
            pltpu.VMEM((BLOCKS + 1, F_W, TILE), f32),
            pltpu.VMEM((F_DEV, F_W, V_F), bf16),
        ],
        compiler_params=params(20),
        cost_estimate=cost(3),
        name="spread_two",
    )(me, counts, rows, cols, *h, tiles)


def relu_mix(me, parts, w_ref):
    weight = jnp.concatenate(
        [
            w_ref[pl.ds(pl.multiple_of(((me + F_DEV - k) % F_DEV) * F_W, F_W), F_W), :]
            for k in range(F_DEV)
        ],
        axis=0,
    )
    s = jnp.concatenate(parts, axis=0)
    return jnp.maximum(jnp.dot(weight.T, s, preferred_element_type=f32), 0.0)


def mix_one_kernel(me_ref, *refs):
    me = me_ref[0]
    in_refs, w_ref, whole_ref, out_refs = refs[:4], refs[4], refs[5], refs[6:]
    for k in range(F_DEV):
        start = pl.multiple_of(((me + F_DEV - k) % F_DEV) * F_W, F_W)
        whole_ref[pl.ds(start, F_W), :] = in_refs[k][0]
    mixed = relu_mix(me, [r[1] for r in in_refs], w_ref)
    whole_ref[...] = (whole_ref[...].astype(f32) + mixed).astype(bf16)
    for k in range(F_DEV):
        start = pl.multiple_of(((me + k) % F_DEV) * F_W, F_W)
        out_refs[k][...] = whole_ref[pl.ds(start, F_W), :]


def mix_one(me, parts, w):
    first, *rest = pl.pallas_call(
        mix_one_kernel,
        in_specs=[SMEM] + [VMEM] * 5,
        out_specs=[VMEM] * 5,
        out_shape=[jax.ShapeDtypeStruct((D, V_F), bf16)] + [CHUNK] * F_DEV,
        compiler_params=params(16),
        cost_estimate=cost(1),
        name="mix_one",
    )(me, *parts, w)
    return first, rest


def mix_two_kernel(last, me_ref, *refs):
    me = me_ref[0]
    s_refs, h_ref, w_ref, out_ref = refs[:4], refs[4], refs[5], refs[-1]
    mixed = relu_mix(me, [r[...] for r in s_refs], w_ref)
    h = (h_ref[...].astype(f32) + mixed).astype(bf16).T.reshape(S_DEV, V_S, D)
    if last:
        out_ref[:, :V_S, :] = refs[6][...]
        out_ref[:, V_S:, :] = h
    else:
        out_ref[...] = h


def mix_two(me, s, h, w, before):
    last = len(before)
    return pl.pallas_call(
        functools.partial(mix_two_kernel, last),
        in_specs=[SMEM] + [VMEM] * (6 + last),
        out_specs=VMEM,
        out_shape=jax.ShapeDtypeStruct((S_DEV, V_S * (1 + last), D), bf16),
        compiler_params=params(16),
        cost_estimate=cost(1),
        name="mix_two",
    )(me, *s, h, w, *before)


def attend_kernel(wq_ref, wk_ref, wv_ref, wo_ref, *refs):
    *h_refs, out_ref, hs, es, qt, vt, ks, ct = refs
    rows = SNAPS * V_S
    for parity in range(2):
        half = h_refs[parity][...] if len(h_refs) == 2 else h_refs[0][:, parity * V_S : (parity + 1) * V_S, :]
        for k in range(2):
            hs[k, parity] = half[:, :, k * 128 : (k + 1) * 128].reshape(S_DEV * V_S, 128).astype(f32)
    wqt = wq_ref[...].T
    wvt = wv_ref[...].T

    def project(c, _):
        at = pl.ds(pl.multiple_of(c * 4 * SNAPS, 4 * SNAPS), 4 * SNAPS)
        x = jnp.concatenate(
            [
                jnp.concatenate(
                    [hs[k, parity, pl.ds(c * 4 + v, S_DEV, stride=V_S), :] for k in range(2)], axis=1
                ).astype(bf16)
                for v in range(4)
                for parity in range(2)
            ],
            axis=0,
        )
        qt[:, at] = lax.dot_general(wqt, x, NT, preferred_element_type=f32).astype(bf16)
        vt[:, at] = lax.dot_general(wvt, x, NT, preferred_element_type=f32).astype(bf16)
        ks[at, :] = jnp.dot(x, wk_ref[...], preferred_element_type=f32).astype(bf16)
        return 0

    lax.fori_loop(0, rows // 512, project, 0, unroll=4)

    def time(dim):
        r = lax.broadcasted_iota(jnp.int32, (SNAPS, SNAPS), dim)
        return jnp.where(r < S_DEV, 2 * r, 2 * r - (SNAPS - 1))

    causal = time(0) <= time(1)
    scale = HEAD_DIM**-0.5 * LOG2_E

    def vertex(v, _):
        at = pl.ds(pl.multiple_of(v * SNAPS, SNAPS), SNAPS)
        key = ks[at, :]

        def padded(h):
            parts = [qt[h * HEAD_DIM : (h + 1) * HEAD_DIM, at]]
            if h > 0:
                parts.insert(0, jnp.zeros((h * HEAD_DIM, SNAPS), bf16))
            if h < HEADS - 1:
                parts.append(jnp.zeros((D - (h + 1) * HEAD_DIM, SNAPS), bf16))
            return jnp.concatenate(parts, axis=0)

        for pair in range(HEADS // 2):
            q_pair = jnp.concatenate([padded(2 * pair), padded(2 * pair + 1)], axis=1)
            scores = jnp.dot(key, q_pair, preferred_element_type=f32)
            for k in range(2):
                head = slice((2 * pair + k) * HEAD_DIM, (2 * pair + k + 1) * HEAD_DIM)
                s = jnp.where(causal, scores[:, k * SNAPS : (k + 1) * SNAPS], masked_score)
                top = jnp.max(s, axis=0, keepdims=True)
                lifted = jnp.exp2((s - top) * scale)
                total = jnp.sum(lifted, axis=0, keepdims=True)
                weights = (lifted * (1.0 / total)).astype(bf16)
                ct[head, at] = jnp.dot(
                    vt[head, at], weights, preferred_element_type=f32
                ).astype(bf16)
        return 0

    lax.fori_loop(0, V_S, vertex, 0, unroll=8)
    low = lax.broadcasted_iota(jnp.int32, (S_DEV, 128), 1) < F_W
    for v in range(V_S):
        at = pl.ds(v, S_DEV, stride=V_S)
        mixed = jnp.dot(
            ct[:, v * SNAPS : (v + 1) * SNAPS].T, wo_ref[...], preferred_element_type=f32
        )
        for k in range(2):
            even = hs[k, 0, at, :] + mixed[:S_DEV, k * 128 : (k + 1) * 128]
            odd = hs[k, 1, at, :] + mixed[S_DEV:, k * 128 : (k + 1) * 128]
            es[2 * k, at, :] = jnp.where(low, even, pltpu.roll(odd, F_W, 1))
            es[2 * k + 1, at, :] = jnp.where(low, pltpu.roll(even, F_W, 1), odd)
    for f in range(F_DEV):
        out_ref[f] = es[f].reshape(S_DEV, V_S, 128).astype(bf16)


def attend(wq, wk, wv, wo, *hidden):
    rows = SNAPS * V_S
    return pl.pallas_call(
        attend_kernel,
        out_shape=jax.ShapeDtypeStruct((F_DEV, S_DEV, V_S, 2 * F_W), bf16),
        scratch_shapes=[
            pltpu.VMEM((2, 2, S_DEV * V_S, 128), f32),
            pltpu.VMEM((F_DEV, S_DEV * V_S, 128), f32),
            pltpu.VMEM((D, rows), bf16),
            pltpu.VMEM((D, rows), bf16),
            pltpu.VMEM((rows, D), bf16),
            pltpu.VMEM((D, rows), bf16),
        ],
        compiler_params=params(32),
        name="attend",
    )(wq, wk, wv, wo, *hidden)


def place_kernel(in_ref, out_ref):
    for g in range(16):
        block = in_ref[g * 8 : (g + 1) * 8].reshape(128, 128).T
        out_ref[0, :, g * 128 : (g + 1) * 128] = block[:F_W]
        out_ref[1, :, g * 128 : (g + 1) * 128] = block[F_W:]


def place(pieces):
    return pl.pallas_call(
        place_kernel,
        grid=(2,),
        in_specs=[pl.BlockSpec((S_DEV * 2, V_S, 2 * F_W), lambda g: (g, 0, 0))],
        out_specs=pl.BlockSpec((2, F_W, V_F * 2), lambda g: (0, 0, g)),
        out_shape=jax.ShapeDtypeStruct((2, F_W, VERT), bf16),
        compiler_params=params(24),
        name="place",
    )(pieces)


def on_device(
    node_features,
    tile_rows,
    tile_cols,
    tile_counts,
    tile_values,
    layer_one,
    layer_two,
    query_weight,
    key_weight,
    value_weight,
    out_weight,
):
    x = jnp.swapaxes(node_features, 1, 2)
    me = lax.axis_index("feat").astype(jnp.int32).reshape(1)
    lists = (tile_values, tile_rows, tile_cols, tile_counts)

    both = range(2)
    s_one = [turn(spread_one(t, me, x, *lists)) for t in both]
    ones = [mix_one(me, s_one[t], layer_one) for t in both]
    h_one = [turn(ones[t][1]) for t in both]
    s_two = [turn(spread_two(t, me, h_one[t], *lists)) for t in both]
    hidden = []
    for t in both:
        hidden = [mix_two(me, s_two[t], ones[t][0], layer_two, hidden)]
    owned = lax.all_to_all(hidden[0], "snap", split_axis=0, concat_axis=0, tiled=True)
    evolved = attend(query_weight, key_weight, value_weight, out_weight, owned)
    pieces = lax.all_to_all(
        evolved.reshape(F_DEV * S_DEV, V_S, 2 * F_W),
        ("feat", "snap"),
        split_axis=0,
        concat_axis=0,
        tiled=True,
    )
    return jnp.swapaxes(place(pieces), 1, 2)


def solution(mesh):
    placed = (
        P("snap", None, "feat"),
        P("snap", None),
        P("snap", None),
        P("snap"),
        P("snap", None, None, None),
        P(),
        P(),
        P(),
        P(),
        P(),
        P(),
    )
    return jax.shard_map(
        on_device, mesh=mesh, in_specs=placed, out_specs=P("snap", None, "feat"), check_vma=False
    )
```
